32 devices in a mesh: groups: 2 (over y), ep: 8 (over z, x), tp: 2 (over core).
Axes of the slice: x: 2, y: 2, z: 4, core: 2. Of those that a mesh axis runs over, the one named last changes fastest.
Arguments:
- hidden: bfloat16 [2, 128, 3584], P(None, ('groups', 'ep')), parts along dimension 1, may hold values from -6 to 6
- norm_gain: bfloat16 [3584], replicated, may hold values from 0.25 to 1.75
- expert_ids: int32 [2, 128, 1], P(None, ('groups', 'ep')), parts along dimension 1, may hold values from 0 to 1, as said below
- shares: float32 [2, 128, 1], P(None, ('groups', 'ep')), parts along dimension 1, may hold values from 0.1 to 1
- slot_index: int32 [2, 128, 1], P(None, ('groups', 'ep')), parts along dimension 1, may hold values from -1 to 3, as said below
- w_gate: bfloat16 [3584, 2048], P(None, ('ep', 'tp')), may hold values from -0.09375 to 0.09375
- w_up: bfloat16 [3584, 2048], P(None, ('ep', 'tp')), may hold values from -0.09375 to 0.09375
- w_down: bfloat16 [2048, 3584], P(('ep', 'tp')), may hold values from -0.1875 to 0.1875
Outputs:
- mixed: bfloat16 [2, 128, 3584], P(None, ('groups', 'ep'), 'tp'), parts along dimension 1
The draws below stay inside these ranges and needn't reach their ends.
There are 2 independent parts, one for each index of `groups`. The reference program is written for one: setup_inputs(seed, part) draws one part's arguments, and reference() takes and returns one part's arrays. A program takes and returns all parts, laid end to end along the dimension named above; an argument that names none is the same for every part. Nothing has to cross between parts.
Inputs may be any that keep to these rules, and one draw needn't show every extreme that they name: `expert_ids`: each row names 1 expert. `slot_index`: -1 marks a dropped choice. Within one micro-batch and one aligned block of 8 rows, the choices naming one expert take slots 0, 1, 2, ... in row order, and a choice is dropped exactly when 4 earlier rows of its block name the same expert.
All inputs are finite; a program needn't handle non-finite values.
Results may differ from the reference program's by a relative error of at most 0.0055.
Values may be sent and summed in bfloat16 or wider, within the bound.
No kernel may reach another device: no remote copies, remote signals or barrier semaphores. Data moves between devices by JAX's collectives and lax.ppermute only.
A program may use at most 64 MiB of HBM per device.

```python
import math
import jax
import jax.numpy as jnp
from jax import lax

D = 3584
FF = 1024
SLICE = 128
MB = 2
ROWS = 8
EXPERTS = 2
TOPK = 1
CAP = 4
ROWS_ALL = 64


def routing_tables(key):
    scores = jax.random.randint(jax.random.fold_in(key, 11), (MB, ROWS_ALL, EXPERTS), 0, 1000)
    favour = jax.random.randint(jax.random.fold_in(key, 12), (EXPERTS,), 0, 800)
    top_one = jax.random.randint(jax.random.fold_in(key, 13), (), 0, EXPERTS)
    block_hot = jax.random.randint(jax.random.fold_in(key, 14), (MB, ROWS_ALL // ROWS), 0, EXPERTS)
    block_rows = jnp.repeat(block_hot, ROWS, axis=1)
    experts = jnp.arange(EXPERTS, dtype=jnp.int32)
    total = scores + favour[None, None, :] + 900 * (experts == top_one).astype(jnp.int32)[None, None, :]
    total = total + 600 * (experts[None, None, :] == block_rows[:, :, None]).astype(jnp.int32)
    total = total * EXPERTS + experts[None, None, :]
    unused, chosen = lax.top_k(total, TOPK)
    chosen = chosen.astype(jnp.int32)
    named = jnp.sum((chosen[..., None] == experts).astype(jnp.int32), axis=2)
    blocks = named.reshape(MB, ROWS_ALL // ROWS, ROWS, EXPERTS)
    ranks = (jnp.cumsum(blocks, axis=2) - blocks).reshape(MB, ROWS_ALL, EXPERTS)
    placed = jnp.take_along_axis(ranks, chosen, axis=2)
    placed = jnp.where(placed < CAP, placed, -1).astype(jnp.int32)
    return (chosen, placed)


def draw_expert_ids(key, part):
    chosen, placed = routing_tables(key)
    return chosen


def draw_slot_index(key, part):
    chosen, placed = routing_tables(key)
    return placed


def block_levels(rng, extent, split, least, high):
    gain = 1.0
    for dim, parts in split:
        draws = jax.random.uniform(jax.random.fold_in(jax.random.fold_in(rng, 6), dim), (parts,), jnp.float32, least / len(split), high / len(split))
        gain = gain * jnp.repeat(jnp.exp(draws), extent[dim] // parts).reshape((-1,) + (1,) * (len(extent) - 1 - dim))
    return gain


def centred(stream_key, extent, spread, most, cuts=(), kind=jnp.bfloat16):
    drawn = spread * jax.random.normal(stream_key, extent, jnp.float32)
    if cuts:
        drawn = drawn * block_levels(stream_key, extent, cuts, -0.22, 0.18)
    return jnp.clip(drawn, -most, most).astype(kind)


def setup_inputs(seed: int = 0, part: int = 0) -> dict:
    key_of = jax.random.split(jax.random.key(seed), 9)
    own_keys = jax.random.split(jax.random.fold_in(key_of[8], part), 9)
    return {
        "hidden": centred(own_keys[0], (MB, ROWS_ALL, D), 1.0, 6.0, ((1, 8),)),
        "norm_gain": jnp.clip(1.0 + 0.15 * jax.random.normal(key_of[1], (D,), jnp.float32), 0.25, 1.75).astype(jnp.bfloat16),
        "expert_ids": draw_expert_ids(jax.random.fold_in(jax.random.fold_in(key_of[8], part), 71), part),
        "shares": jnp.clip(jnp.exp(math.log(1.0) - 2.3025851 * jax.random.uniform(own_keys[3], (MB, ROWS_ALL, TOPK), jnp.float32) ** block_levels(own_keys[3], (MB, ROWS_ALL, TOPK), ((1, 8),), -0.2, 0.2)), 0.1, 1.0),
        "slot_index": draw_slot_index(jax.random.fold_in(jax.random.fold_in(key_of[8], part), 71), part),
        "w_gate": centred(key_of[5], (D, EXPERTS * FF), D ** -0.5, 0.09375, ((1, 16),)),
        "w_up": centred(key_of[6], (D, EXPERTS * FF), D ** -0.5, 0.09375, ((1, 16),)),
        "w_down": centred(key_of[7], (EXPERTS * FF, D), FF ** -0.5, 0.1875, ((0, 16),)),
    }


def reference(hidden, norm_gain, expert_ids, shares, slot_index, w_gate, w_up, w_down):
    sources = ROWS_ALL // ROWS
    per_expert = sources * CAP
    total_slots = EXPERTS * per_expert
    pieces = FF // SLICE
    results = []
    for micro_batch in range(MB):
        values = hidden[micro_batch].astype(jnp.float32)
        scale = lax.rsqrt(lax.optimization_barrier(jnp.mean(values * values, axis=-1, keepdims=True)) + 1e-06)
        normed = (values * scale * norm_gain.astype(jnp.float32)).astype(jnp.bfloat16)
        chosen = expert_ids[micro_batch]
        placed = slot_index[micro_batch]
        anchor = (jnp.arange(ROWS_ALL, dtype=jnp.int32) // ROWS)[:, None]
        kept = placed >= 0
        position = jnp.where(kept, (chosen * sources + anchor) * CAP + placed, total_slots).astype(jnp.int32)
        row_ids = jnp.broadcast_to(jnp.arange(ROWS_ALL, dtype=jnp.int32)[:, None], position.shape)
        row_table = jnp.zeros((total_slots + 1,), jnp.int32).at[position.reshape(-1)].set(row_ids.reshape(-1))

        def expert_out(expert):
            start = expert.astype(jnp.int32)
            picks = lax.dynamic_slice_in_dim(row_table, start * per_expert, per_expert)
            inputs = normed[picks]
            gate_cols = lax.dynamic_slice_in_dim(w_gate, start * FF, FF, 1)
            up_cols = lax.dynamic_slice_in_dim(w_up, start * FF, FF, 1)
            gate_val = jnp.dot(inputs, gate_cols, preferred_element_type=jnp.float32)
            up_val = jnp.dot(inputs, up_cols, preferred_element_type=jnp.float32)
            active = (jax.nn.silu(gate_val) * up_val).astype(jnp.bfloat16)
            down_rows = lax.dynamic_slice_in_dim(w_down, start * FF, FF, 0).reshape(pieces, SLICE, D)
            partial_value = jnp.einsum('rps,psd->rpd', active.reshape(per_expert, pieces, SLICE).astype(jnp.float32), down_rows.astype(jnp.float32))
            partial_value = partial_value.astype(jnp.bfloat16)
            return lax.optimization_barrier(jnp.sum(partial_value.astype(jnp.float32), axis=1))
        outputs = lax.map(expert_out, jnp.arange(EXPERTS, dtype=jnp.int32))
        outputs = jnp.concatenate([outputs.reshape(total_slots, D), jnp.zeros((1, D), jnp.float32)], 0)
        picked = outputs[position]
        weights = shares[micro_batch] * kept.astype(jnp.float32)
        routed = jnp.einsum('rk,rkd->rd', weights, picked)
        results.append((values + routed).astype(jnp.bfloat16))
    return jnp.stack(results)
```

```python
import functools

import jax
import jax.numpy as jnp
from jax import lax
from jax.experimental import pallas as pl
from jax.experimental.pallas import tpu as pltpu
from jax.sharding import PartitionSpec as P

FF = 1024
SLICE = 128


def hits(ids, placed, node, nodes, first, slots, micro_batch, capacity):
    per_node = slots[1]
    row_count = ids.shape[1]
    slot = lax.broadcasted_iota(jnp.int32, (slots[0] * per_node, row_count), 0) + first * per_node
    offset = ids - node
    offset = jnp.where(offset < 0, offset + nodes, offset)
    place = offset * per_node + micro_batch * capacity + placed
    place = jnp.where(placed >= 0, place, -1)
    return [slot == place[k : k + 1, :] for k in range(ids.shape[0])]


def dispatch_kernel(sizes, hidden_ref, gain_ref, ids_ref, placed_ref, own_ref, rest_ref):
    nodes, node_size, capacity, half, cut = sizes
    micro_count = hidden_ref.shape[0]
    per_node = micro_count * capacity
    node = lax.axis_index("ep") // node_size
    gain = gain_ref[...].astype(jnp.float32)
    own = rest = 0.0
    for m in range(micro_count):
        values = hidden_ref[m].astype(jnp.float32)
        scale = lax.rsqrt(jnp.mean(values * values, axis=-1, keepdims=True) + 1e-06)
        normed = (values * scale * gain).astype(jnp.bfloat16)

        def select(first, count):
            chosen = hits(
                ids_ref[m], placed_ref[m], node, nodes, first, (count, per_node), m, capacity
            )
            flags = functools.reduce(jnp.logical_or, chosen)
            return jnp.dot(
                jnp.where(flags, 1.0, 0.0).astype(jnp.bfloat16),
                normed,
                preferred_element_type=jnp.float32,
            )

        own = own + select(0, 1)
        rest = rest + select(1, nodes - 1)
    own_ref[...] = own.astype(jnp.bfloat16)
    rest_ref[...] = rest.astype(jnp.bfloat16)


def expert_kernel(sizes, *refs):
    node_size, half = sizes
    pieces = refs[: 2 * node_size]
    gate_ref, up_ref, down_ref, keep_ref, send_ref = refs[2 * node_size :]
    core = lax.axis_index("tp")
    rows = jnp.concatenate([ref[...].astype(jnp.float32) for ref in pieces], 0).astype(jnp.bfloat16)
    gate_val = jnp.dot(rows, gate_ref[...], preferred_element_type=jnp.float32)
    up_val = jnp.dot(rows, up_ref[...], preferred_element_type=jnp.float32)
    active = (gate_val / (1.0 + jnp.exp(-gate_val)) * up_val).astype(jnp.bfloat16)

    def down(which):
        columns = pl.ds(pl.multiple_of(which * half, 128), half)
        return jnp.dot(active, down_ref[:, columns], preferred_element_type=jnp.float32)

    send_ref[...] = down(1 - core).astype(jnp.bfloat16).reshape(send_ref.shape)
    keep_ref[...] = down(core).reshape(keep_ref.shape)


def add_cores_kernel(sizes, keep_ref, got_ref, *out_refs):
    node_size, per_node = sizes
    for k in range(node_size):
        total = keep_ref[k] + got_ref[k].astype(jnp.float32)
        own_ref, rest_ref = out_refs[2 * k : 2 * k + 2]
        own_ref[...] = total[:per_node].astype(own_ref.dtype)
        rest_ref[...] = total[per_node:].astype(rest_ref.dtype)


def add_members_kernel(*refs):
    total = refs[0][...]
    for ref in refs[1:-1]:
        total = total + ref[...].astype(jnp.float32)
    refs[-1][...] = total.astype(jnp.bfloat16)


def combine_kernel(sizes, hidden_ref, ids_ref, placed_ref, shares_ref, *refs):
    nodes, node_size, capacity, half = sizes
    own_refs, rest_ref, out_ref = refs[:node_size], refs[node_size], refs[node_size + 1]
    micro_count = hidden_ref.shape[0]
    per_node = micro_count * capacity
    node = lax.axis_index("ep") // node_size
    core = lax.axis_index("tp")
    own = own_refs[0][...]
    for ref in own_refs[1:]:
        own = own + ref[...].astype(jnp.float32)
    rest = rest_ref[...].astype(jnp.float32)
    columns = pl.ds(pl.multiple_of(core * half, 128), half)
    for m in range(micro_count):
        total = hidden_ref[m, :, columns].astype(jnp.float32)
        for first, count, block in ((0, 1, own), (1, nodes - 1, rest)):
            chosen = hits(
                ids_ref[m], placed_ref[m], node, nodes, first, (count, per_node), m, capacity
            )
            weights = sum(
                jnp.where(flags, shares_ref[m][k : k + 1, :], 0.0) for k, flags in enumerate(chosen)
            )
            total = total + lax.dot_general(
                weights,
                block,
                (((0,), (0,)), ((), ())),
                precision=lax.Precision.HIGHEST,
                preferred_element_type=jnp.float32,
            )
        out_ref[m] = total.astype(jnp.bfloat16)


def per_device(hidden, norm_gain, expert_ids, shares, slot_index, w_gate, w_up, w_down):
    micro_count, row_count, model_width = hidden.shape
    ep_count = lax.axis_size("ep")
    share_count = lax.axis_size("tp")
    node_size = FF // SLICE // share_count
    nodes = ep_count // node_size
    capacity = row_count * expert_ids.shape[2] // nodes
    half = model_width // share_count
    per_node = micro_count * capacity
    rest_rows = (nodes - 1) * per_node
    ids, placed, weights = (jnp.swapaxes(a, 1, 2) for a in (expert_ids, slot_index, shares))
    params = pltpu.CompilerParams(
        vmem_limit_bytes=(16 if nodes * per_node <= 32 else 56) * 1024 * 1024
    )
    bf16, f32 = jnp.bfloat16, jnp.float32

    def call(kernel, outs, *args):
        return pl.pallas_call(
            kernel,
            out_shape=[jax.ShapeDtypeStruct(shape, kind) for shape, kind in outs],
            compiler_params=params,
        )(*args)

    def to_member(array, k):
        pairs = [(j, j // node_size * node_size + (j % node_size ^ k)) for j in range(ep_count)]
        return lax.ppermute(array, "ep", pairs)

    def to_nodes(array, sign):
        blocks = []
        for n in range(1, nodes):
            block = array if nodes == 2 else array[(n - 1) * per_node : n * per_node]
            pairs = [(j, (j + sign * n * node_size) % ep_count) for j in range(ep_count)]
            blocks.append(lax.ppermute(block, "ep", pairs))
        return blocks[0] if nodes == 2 else jnp.concatenate(blocks, 0)

    own, rest = call(
        functools.partial(dispatch_kernel, (nodes, node_size, capacity, half, False)),
        [((per_node, model_width), bf16), ((rest_rows, model_width), bf16)],
        hidden,
        norm_gain[None],
        ids,
        placed,
    )
    inbox = to_nodes(rest, 1)
    owns = [own] + [to_member(own, k) for k in range(1, node_size)]
    rests = [inbox] + [to_member(inbox, k) for k in range(1, node_size)]
    pieces = [piece for pair in zip(owns, rests) for piece in pair]
    blocks = (node_size, nodes * per_node, half)
    keep, send = call(
        functools.partial(expert_kernel, (node_size, half)),
        [(blocks, f32), (blocks, bf16)],
        *pieces,
        w_gate,
        w_up,
        w_down,
    )
    got = lax.ppermute(send, "tp", [(i, (i + 1) % share_count) for i in range(share_count)])
    sums = call(
        functools.partial(add_cores_kernel, (node_size, per_node)),
        [
            ((count, half), kind)
            for kind in [f32] + [bf16] * (node_size - 1)
            for count in (per_node, rest_rows)
        ],
        keep,
        got,
    )
    away = [sums[1]] + [to_member(sums[2 * k + 1], k) for k in range(1, node_size)]
    home = [sums[0]] + [to_member(sums[2 * k], k) for k in range(1, node_size)]
    (outbox,) = call(add_members_kernel, [((rest_rows, half), bf16)], *away)
    returned = to_nodes(outbox, -1)
    (mixed,) = call(
        functools.partial(combine_kernel, (nodes, node_size, capacity, half)),
        [((micro_count, row_count, half), bf16)],
        hidden,
        ids,
        placed,
        weights,
        *home,
        returned,
    )
    return mixed


def solution(mesh):
    in_specs = (
        P(None, ("groups", "ep"), None),
        P(),
        P(None, ("groups", "ep"), None),
        P(None, ("groups", "ep"), None),
        P(None, ("groups", "ep"), None),
        P(None, ("ep", "tp")),
        P(None, ("ep", "tp")),
        P(("ep", "tp"), None),
    )
    out_specs = P(None, ("groups", "ep"), "tp")
    return jax.shard_map(
        per_device, mesh=mesh, in_specs=in_specs, out_specs=out_specs, check_vma=False
    )
```

```python
import functools

import jax
import jax.numpy as jnp
from jax import lax
from jax.experimental import pallas as pl
from jax.experimental.pallas import tpu as pltpu
from jax.sharding import PartitionSpec as P

FF = 1024
SLICE = 128
BF16 = jnp.bfloat16
F32 = jnp.float32


def hits(ids, placed, sizes, node, micro_batch, first, count):
    nodes, capacity, per_node = sizes
    slot = lax.broadcasted_iota(jnp.int32, (count * per_node, ids.shape[1]), 0) + first * per_node
    offset = ids - node
    offset = jnp.where(offset < 0, offset + nodes, offset)
    place = jnp.where(placed >= 0, offset * per_node + micro_batch * capacity + placed, -1)
    return [slot == place[k : k + 1, :] for k in range(ids.shape[0])]


def picks_kernel(sizes, node_size, ids_ref, placed_ref, picks_ref):
    node = lax.axis_index("ep") // node_size
    for m in range(ids_ref.shape[0]):
        flags = hits(ids_ref[m], placed_ref[m], sizes, node, m, 0, sizes[0])
        flags = functools.reduce(jnp.logical_or, flags)
        picks_ref[m] = jnp.where(flags, 1.0, 0.0)


def dispatch_kernel(hidden_ref, gain_ref, picks_ref, own_ref, rest_ref):
    gain = gain_ref[...].astype(F32).reshape(1, -1)
    slots = 0.0
    for m in range(hidden_ref.shape[0]):
        values = hidden_ref[m].astype(F32)
        scale = lax.rsqrt(jnp.mean(values * values, axis=-1, keepdims=True) + 1e-06)
        normed = (values * scale * gain).astype(BF16)
        slots = slots + jnp.dot(picks_ref[m].astype(BF16), normed, preferred_element_type=F32)
    per_node = own_ref.shape[0]
    own_ref[...] = slots[:per_node].astype(BF16)
    rest_ref[...] = slots[per_node:].astype(BF16)


def table_kernel(sizes, node_size, ids_ref, placed_ref, shares_ref, table_ref):
    node = lax.axis_index("ep") // node_size
    for m in range(ids_ref.shape[0]):
        flags = hits(ids_ref[m], placed_ref[m], sizes, node, m, 0, sizes[0])
        table = sum(
            jnp.where(flag, shares_ref[m][k : k + 1, :], 0.0) for k, flag in enumerate(flags)
        )
        table_ref[m] = table.T


def join_kernel(own_ref, inbox_ref, mine_ref):
    mine_ref[...] = jnp.concatenate(
        [own_ref[...].astype(F32), inbox_ref[...].astype(F32)], 0
    ).astype(BF16)


def expert_kernel(
    mine_ref,
    first_ref,
    second_ref,
    far_ref,
    gate_ref,
    up_ref,
    down_ref,
    keep_ref,
    send_ref,
    rows_ref,
):
    core = lax.axis_index("tp")
    half = keep_ref.shape[2]
    rows_ref[0] = mine_ref[...]
    rows_ref[1 + core] = first_ref[...]
    rows_ref[2 - core] = second_ref[...]
    rows_ref[3] = far_ref[...]
    rows = rows_ref[...].reshape(-1, rows_ref.shape[2])
    gate_val = jnp.dot(rows, gate_ref[...], preferred_element_type=F32)
    up_val = jnp.dot(rows, up_ref[...], preferred_element_type=F32)
    active = (gate_val / (1.0 + jnp.exp(-gate_val)) * up_val).astype(BF16)

    def down(which):
        columns = pl.ds(pl.multiple_of(which * half, 128), half)
        return jnp.dot(active, down_ref[:, columns], preferred_element_type=F32)

    send_ref[...] = down(1 - core).astype(BF16).reshape(send_ref.shape)
    keep_ref[...] = down(core).reshape(keep_ref.shape)


def add_cores_kernel(keep_ref, got_ref, far_ref, second_ref, first_ref, mine_ref):
    core = lax.axis_index("tp")

    def total(k):
        return keep_ref[k] + got_ref[k].astype(F32)

    far_ref[...] = total(3).astype(BF16)
    second_ref[...] = total(2 - core).astype(BF16)
    first_ref[...] = total(1 + core)
    mine_ref[...] = total(0)


def pass_on_kernel(first_ref, got_ref, out_ref):
    out_ref[...] = (first_ref[...] + got_ref[...].astype(F32)).astype(BF16)


def members_kernel(mine_ref, first_ref, second_ref, own_ref, outbox_ref):
    total = mine_ref[...] + first_ref[...].astype(F32) + second_ref[...].astype(F32)
    per_node = own_ref.shape[0]
    own_ref[...] = total[:per_node]
    outbox_ref[...] = total[per_node:].astype(BF16)


def weighted(base, weights, block, sizes, micro_batch, first, count):
    nodes, capacity, per_node = sizes
    for n in range(count):
        for c in range(capacity):
            slot = n * per_node + micro_batch * capacity + c
            column = first * per_node + slot
            base = base + weights[:, column : column + 1] * block[slot : slot + 1, :]
    return base


def own_kernel(sizes, hidden_ref, weights_ref, own_ref, out_ref):
    own = own_ref[...]
    half = out_ref.shape[2]
    columns = pl.ds(pl.multiple_of(lax.axis_index("tp") * half, 128), half)
    for m in range(hidden_ref.shape[0]):
        base = hidden_ref[m, :, columns].astype(F32)
        out_ref[m] = weighted(base, weights_ref[m], own, sizes, m, 0, 1)


def rest_kernel(sizes, base_ref, weights_ref, rest_ref, out_ref):
    rest = rest_ref[...].astype(F32)
    for m in range(base_ref.shape[0]):
        out_ref[m] = weighted(base_ref[m], weights_ref[m], rest, sizes, m, 1, sizes[0] - 1).astype(
            BF16
        )


def per_device(hidden, norm_gain, expert_ids, shares, slot_index, w_gate, w_up, w_down):
    micro_count, row_count, model_width = hidden.shape
    top_count = expert_ids.shape[2]
    ep_count = lax.axis_size("ep")
    share_count = lax.axis_size("tp")
    node_size = FF // SLICE // share_count
    nodes = ep_count // node_size
    capacity = row_count * top_count // nodes
    half = model_width // share_count
    per_node = micro_count * capacity
    all_rows = nodes * per_node
    rest_rows = all_rows - per_node
    sizes = (nodes, capacity, per_node)
    ids, placed, weights = (jnp.swapaxes(a, 1, 2) for a in (expert_ids, slot_index, shares))
    small = all_rows <= 32
    params = pltpu.CompilerParams(vmem_limit_bytes=(16 if small else 56) * 1024 * 1024)

    def call(kernel, outs, *args, scratch=(), cost=0):
        return pl.pallas_call(
            kernel,
            out_shape=[jax.ShapeDtypeStruct(shape, kind) for shape, kind in outs],
            scratch_shapes=scratch,
            compiler_params=params,
            cost_estimate=pl.CostEstimate(flops=cost, bytes_accessed=cost // 500, transcendentals=0),
        )(*args)

    def to_first(array):
        return to_partner(array, lambda core: 1 + core)

    def to_second(array):
        return to_partner(array, lambda core: 2 - core)

    def to_partner(array, flip):
        pairs = []
        for j in range(ep_count):
            for core in range(share_count):
                other = j // node_size * node_size + (j % node_size ^ flip(core))
                pairs.append((j * share_count + core, other * share_count + core))
        return lax.ppermute(array, ("ep", "tp"), pairs)

    def to_nodes(array, sign):
        blocks = []
        for n in range(1, nodes):
            block = array if nodes == 2 else array[(n - 1) * per_node : n * per_node]
            pairs = [(j, (j + sign * n * node_size) % ep_count) for j in range(ep_count)]
            blocks.append(lax.ppermute(block, "ep", pairs))
        return blocks[0] if nodes == 2 else jnp.concatenate(blocks, 0)

    (picks,) = call(
        functools.partial(picks_kernel, sizes, node_size),
        [((micro_count, all_rows, row_count), F32)],
        ids,
        placed,
        cost=3 * 10**9,
    )
    own, rest = call(
        dispatch_kernel,
        [((per_node, model_width), BF16), ((rest_rows, model_width), BF16)],
        hidden,
        norm_gain,
        picks,
        cost=20 * 10**9,
    )
    (table,) = call(
        functools.partial(table_kernel, sizes, node_size),
        [((micro_count, row_count, all_rows), F32)],
        ids,
        placed,
        weights,
    )
    inbox = to_nodes(rest, 1)
    (mine,) = call(join_kernel, [((all_rows, model_width), BF16)], own, inbox)
    first = to_first(mine)
    second = to_second(mine)
    far = to_second(first)
    blocks = (node_size, all_rows, half)
    keep, send = call(
        expert_kernel,
        [(blocks, F32), (blocks, BF16)],
        mine,
        first,
        second,
        far,
        w_gate,
        w_up,
        w_down,
        scratch=[pltpu.VMEM((node_size, all_rows, model_width), BF16)],
        cost=10**6,
    )
    got = lax.ppermute(send, "tp", [(i, (i + 1) % share_count) for i in range(share_count)])
    block = (all_rows, half)
    far_sum, second_sum, first_sum, mine_sum = call(
        add_cores_kernel, [(block, BF16), (block, BF16), (block, F32), (block, F32)], keep, got
    )
    far_got = to_second(far_sum)
    second_got = to_second(second_sum)
    (first_sum,) = call(pass_on_kernel, [(block, BF16)], first_sum, far_got)
    first_got = to_first(first_sum)
    own_sum, outbox = call(
        members_kernel,
        [((per_node, half), F32), ((rest_rows, half), BF16)],
        mine_sum,
        first_got,
        second_got,
    )
    returned = to_nodes(outbox, -1)
    rows = (micro_count, row_count, half)
    (base,) = call(functools.partial(own_kernel, sizes), [(rows, F32)], hidden, table, own_sum)
    (mixed,) = call(functools.partial(rest_kernel, sizes), [(rows, BF16)], base, table, returned)
    return mixed


def solution(mesh):
    in_specs = (
        P(None, ("groups", "ep"), None),
        P(),
        P(None, ("groups", "ep"), None),
        P(None, ("groups", "ep"), None),
        P(None, ("groups", "ep"), None),
        P(None, ("ep", "tp")),
        P(None, ("ep", "tp")),
        P(("ep", "tp"), None),
    )
    out_specs = P(None, ("groups", "ep"), "tp")
    return jax.shard_map(
        per_device, mesh=mesh, in_specs=in_specs, out_specs=out_specs, check_vma=False
    )
```

```python
import functools

import jax
import jax.numpy as jnp
from jax import lax
from jax.experimental import pallas as pl
from jax.experimental.pallas import tpu as pltpu
from jax.sharding import PartitionSpec as P

FF = 1024
SLICE = 128
BF16 = jnp.bfloat16
F32 = jnp.float32


def hits(ids, placed, slot, sizes, node, micro_batch):
    nodes, capacity, per_node = sizes
    offset = ids - node
    offset = jnp.where(offset < 0, offset + nodes, offset)
    place = jnp.where(placed >= 0, offset * per_node + micro_batch * capacity + placed, -1)
    return [slot == place[k : k + 1, :] for k in range(ids.shape[0])]


def slots_kernel(slot_ref):
    slot_ref[...] = lax.broadcasted_iota(jnp.int32, slot_ref.shape, 0)


def dispatch_kernel(
    sizes, node_size, slot_ref, hidden_ref, gain_ref, ids_ref, placed_ref, own_ref, rest_ref
):
    node = lax.axis_index("ep") // node_size
    gain = gain_ref[...].astype(F32).reshape(1, -1)
    slots = 0.0
    for m in range(hidden_ref.shape[0]):
        flags = hits(ids_ref[m], placed_ref[m], slot_ref[...], sizes, node, m)
        picks = jnp.where(functools.reduce(jnp.logical_or, flags), 1.0, 0.0).astype(BF16)
        values = hidden_ref[m].astype(F32)
        scale = lax.rsqrt(jnp.mean(values * values, axis=-1, keepdims=True) + 1e-06)
        normed = (values * scale * gain).astype(BF16)
        slots = slots + jnp.dot(picks, normed, preferred_element_type=F32)
    per_node = own_ref.shape[0]
    own_ref[...] = slots[:per_node].astype(BF16)
    rest_ref[...] = slots[per_node:].astype(BF16)


def table_kernel(sizes, node_size, slot_ref, ids_ref, placed_ref, shares_ref, table_ref):
    node = lax.axis_index("ep") // node_size
    for m in range(ids_ref.shape[0]):
        flags = hits(ids_ref[m], placed_ref[m], slot_ref[...], sizes, node, m)
        table = sum(
            jnp.where(flag, shares_ref[m][k : k + 1, :], 0.0) for k, flag in enumerate(flags)
        )
        table_ref[m] = table.T


def expert_kernel(*refs):
    pieces, (gate_ref, up_ref, down_ref, keep_ref, send_ref) = refs[:-5], refs[-5:]
    core = lax.axis_index("tp")
    half = keep_ref.shape[2]
    rows = jnp.concatenate([ref[...].astype(F32) for ref in pieces], 0).astype(BF16)
    gate_val = jnp.dot(rows, gate_ref[...], preferred_element_type=F32)
    up_val = jnp.dot(rows, up_ref[...], preferred_element_type=F32)
    active = (gate_val / (1.0 + jnp.exp(-gate_val)) * up_val).astype(BF16)

    def down(which):
        columns = pl.ds(pl.multiple_of(which * half, 128), half)
        return jnp.dot(active, down_ref[:, columns], preferred_element_type=F32)

    send_ref[...] = down(1 - core).astype(BF16).reshape(send_ref.shape)
    keep_ref[...] = down(core).reshape(keep_ref.shape)


def add_cores_kernel(keep_ref, got_ref, *out_refs):
    for k in range(keep_ref.shape[0]):
        total = keep_ref[k] + got_ref[k].astype(F32)
        own_ref, rest_ref = out_refs[2 * k : 2 * k + 2]
        per_node = own_ref.shape[0]
        own_ref[...] = total[:per_node].astype(own_ref.dtype)
        rest_ref[...] = total[per_node:].astype(rest_ref.dtype)


def add_members_kernel(*refs):
    total = refs[0][...]
    for ref in refs[1:-1]:
        total = total + ref[...].astype(F32)
    refs[-1][...] = total.astype(BF16)


def weighted(base, weights, block, sizes, micro_batch, first, count):
    nodes, capacity, per_node = sizes
    for n in range(count):
        for c in range(capacity):
            slot = n * per_node + micro_batch * capacity + c
            column = first * per_node + slot
            base = base + weights[:, column : column + 1] * block[slot : slot + 1, :]
    return base


def own_kernel(sizes, hidden_ref, weights_ref, *refs):
    own_refs, out_ref = refs[:-1], refs[-1]
    own = own_refs[0][...]
    for ref in own_refs[1:]:
        own = own + ref[...].astype(F32)
    half = out_ref.shape[2]
    columns = pl.ds(pl.multiple_of(lax.axis_index("tp") * half, 128), half)
    for m in range(hidden_ref.shape[0]):
        base = hidden_ref[m, :, columns].astype(F32)
        out_ref[m] = weighted(base, weights_ref[m], own, sizes, m, 0, 1)


def rest_kernel(sizes, base_ref, weights_ref, rest_ref, out_ref):
    rest = rest_ref[...].astype(F32)
    for m in range(base_ref.shape[0]):
        out_ref[m] = weighted(base_ref[m], weights_ref[m], rest, sizes, m, 1, sizes[0] - 1).astype(
            BF16
        )


def per_device(hidden, norm_gain, expert_ids, shares, slot_index, w_gate, w_up, w_down):
    micro_count, row_count, model_width = hidden.shape
    top_count = expert_ids.shape[2]
    ep_count = lax.axis_size("ep")
    share_count = lax.axis_size("tp")
    node_size = FF // SLICE // share_count
    nodes = ep_count // node_size
    capacity = row_count * top_count // nodes
    half = model_width // share_count
    per_node = micro_count * capacity
    all_rows = nodes * per_node
    rest_rows = all_rows - per_node
    sizes = (nodes, capacity, per_node)
    ids, placed, weights = (jnp.swapaxes(a, 1, 2) for a in (expert_ids, slot_index, shares))
    small = all_rows <= 32
    params = pltpu.CompilerParams(vmem_limit_bytes=(16 if small else 56) * 1024 * 1024)

    def call(kernel, outs, *args, scratch=(), cost=0):
        return pl.pallas_call(
            kernel,
            out_shape=[jax.ShapeDtypeStruct(shape, kind) for shape, kind in outs],
            scratch_shapes=scratch,
            compiler_params=params,
            cost_estimate=pl.CostEstimate(flops=cost, bytes_accessed=cost // 500, transcendentals=0),
        )(*args)

    def to_member(array, k):
        pairs = [(j, j // node_size * node_size + (j % node_size ^ k)) for j in range(ep_count)]
        return lax.ppermute(array, "ep", pairs)

    def to_nodes(array, sign):
        blocks = []
        for n in range(1, nodes):
            block = array if nodes == 2 else array[(n - 1) * per_node : n * per_node]
            pairs = [(j, (j + sign * n * node_size) % ep_count) for j in range(ep_count)]
            blocks.append(lax.ppermute(block, "ep", pairs))
        return blocks[0] if nodes == 2 else jnp.concatenate(blocks, 0)

    (slot,) = call(slots_kernel, [((all_rows, row_count), jnp.int32)], cost=5 * 10**9)
    own, rest = call(
        functools.partial(dispatch_kernel, sizes, node_size),
        [((per_node, model_width), BF16), ((rest_rows, model_width), BF16)],
        slot,
        hidden,
        norm_gain,
        ids,
        placed,
        cost=20 * 10**9,
    )
    (table,) = call(
        functools.partial(table_kernel, sizes, node_size),
        [((micro_count, row_count, all_rows), F32)],
        slot,
        ids,
        placed,
        weights,
    )
    members = range(1, node_size)
    inbox = to_nodes(rest, 1)
    owns = [own] + [to_member(own, k) for k in members]
    rests = [inbox] + [to_member(inbox, k) for k in members]
    blocks = (node_size, all_rows, half)
    keep, send = call(
        expert_kernel,
        [(blocks, F32), (blocks, BF16)],
        *[piece for pair in zip(owns, rests) for piece in pair],
        w_gate,
        w_up,
        w_down,
        cost=10**6,
    )
    got = lax.ppermute(send, "tp", [(i, (i + 1) % share_count) for i in range(share_count)])
    sums = call(
        add_cores_kernel,
        [
            ((count, half), kind)
            for kind in [F32] + [BF16] * (node_size - 1)
            for count in (per_node, rest_rows)
        ],
        keep,
        got,
    )
    away = [sums[1]] + [to_member(sums[2 * k + 1], k) for k in members]
    home = [sums[0]] + [to_member(sums[2 * k], k) for k in members]
    (outbox,) = call(add_members_kernel, [((rest_rows, half), BF16)], *away)
    returned = to_nodes(outbox, -1)
    rows = (micro_count, row_count, half)
    (base,) = call(functools.partial(own_kernel, sizes), [(rows, F32)], hidden, table, *home)
    (mixed,) = call(functools.partial(rest_kernel, sizes), [(rows, BF16)], base, table, returned)
    return mixed


def solution(mesh):
    in_specs = (
        P(None, ("groups", "ep"), None),
        P(),
        P(None, ("groups", "ep"), None),
        P(None, ("groups", "ep"), None),
        P(None, ("groups", "ep"), None),
        P(None, ("ep", "tp")),
        P(None, ("ep", "tp")),
        P(("ep", "tp"), None),
    )
    out_specs = P(None, ("groups", "ep"), "tp")
    return jax.shard_map(
        per_device, mesh=mesh, in_specs=in_specs, out_specs=out_specs, check_vma=False
    )
```

```python
import functools

import jax
import jax.numpy as jnp
from jax import lax
from jax.experimental import pallas as pl
from jax.experimental.pallas import tpu as pltpu
from jax.sharding import PartitionSpec as P

FF = 1024
SLICE = 128
BF16 = jnp.bfloat16
F32 = jnp.float32


def hits(ids, placed, slot, sizes, node, micro_batch):
    nodes, capacity, per_node = sizes
    offset = ids - node
    offset = jnp.where(offset < 0, offset + nodes, offset)
    place = jnp.where(placed >= 0, offset * per_node + micro_batch * capacity + placed, -1)
    return [slot == place[k : k + 1, :] for k in range(ids.shape[0])]


def slots_kernel(slot_ref):
    slot_ref[...] = lax.broadcasted_iota(jnp.int32, slot_ref.shape, 0)


def dispatch_kernel(
    sizes, node_size, slot_ref, hidden_ref, gain_ref, ids_ref, placed_ref, own_ref, rest_ref
):
    node = lax.axis_index("ep") // node_size
    gain = gain_ref[...].astype(F32).reshape(1, -1)
    slots = 0.0
    for m in range(hidden_ref.shape[0]):
        flags = hits(ids_ref[m], placed_ref[m], slot_ref[...], sizes, node, m)
        picks = jnp.where(functools.reduce(jnp.logical_or, flags), 1.0, 0.0).astype(BF16)
        values = hidden_ref[m].astype(F32)
        scale = lax.rsqrt(jnp.mean(values * values, axis=-1, keepdims=True) + 1e-06)
        normed = (values * scale * gain).astype(BF16)
        slots = slots + jnp.dot(picks, normed, preferred_element_type=F32)
    per_node = own_ref.shape[0]
    own_ref[...] = slots[:per_node].astype(BF16)
    rest_ref[...] = slots[per_node:].astype(BF16)


def table_kernel(sizes, node_size, slot_ref, ids_ref, placed_ref, shares_ref, table_ref):
    node = lax.axis_index("ep") // node_size
    for m in range(ids_ref.shape[0]):
        flags = hits(ids_ref[m], placed_ref[m], slot_ref[...], sizes, node, m)
        table = sum(
            jnp.where(flag, shares_ref[m][k : k + 1, :], 0.0) for k, flag in enumerate(flags)
        )
        table_ref[m] = table.T


def expert_kernel(*refs):
    pieces, (gate_ref, up_ref, down_ref, keep_ref, send_ref) = refs[:-5], refs[-5:]
    core = lax.axis_index("tp")
    half = keep_ref.shape[2]
    rows = jnp.concatenate([ref[...].astype(F32) for ref in pieces], 0).astype(BF16)
    gate_val = jnp.dot(rows, gate_ref[...], preferred_element_type=F32)
    up_val = jnp.dot(rows, up_ref[...], preferred_element_type=F32)
    active = (gate_val / (1.0 + jnp.exp(-gate_val)) * up_val).astype(BF16)

    def down(which):
        columns = pl.ds(pl.multiple_of(which * half, 128), half)
        return jnp.dot(active, down_ref[:, columns], preferred_element_type=F32)

    send_ref[...] = down(1 - core).astype(BF16).reshape(send_ref.shape)
    keep_ref[...] = down(core).reshape(keep_ref.shape)


def add_cores_kernel(keep_ref, got_ref, *out_refs):
    for k in range(keep_ref.shape[0]):
        total = keep_ref[k] + got_ref[k].astype(F32)
        own_ref, rest_ref = out_refs[2 * k : 2 * k + 2]
        per_node = own_ref.shape[0]
        own_ref[...] = total[:per_node].astype(own_ref.dtype)
        rest_ref[...] = total[per_node:].astype(rest_ref.dtype)


def add_members_kernel(*refs):
    total = refs[0][...]
    for ref in refs[1:-1]:
        total = total + ref[...].astype(F32)
    refs[-1][...] = total.astype(BF16)


def weighted(base, weights, block, sizes, micro_batch, first, count):
    nodes, capacity, per_node = sizes
    for n in range(count):
        for c in range(capacity):
            slot = n * per_node + micro_batch * capacity + c
            column = first * per_node + slot
            base = base + weights[:, column : column + 1] * block[slot : slot + 1, :]
    return base


def own_kernel(sizes, hidden_ref, weights_ref, *refs):
    own_refs, out_ref = refs[:-1], refs[-1]
    own = own_refs[0][...]
    for ref in own_refs[1:]:
        own = own + ref[...].astype(F32)
    half = out_ref.shape[2]
    columns = pl.ds(pl.multiple_of(lax.axis_index("tp") * half, 128), half)
    for m in range(hidden_ref.shape[0]):
        base = hidden_ref[m, :, columns].astype(F32)
        out_ref[m] = weighted(base, weights_ref[m], own, sizes, m, 0, 1)


def rest_kernel(sizes, base_ref, weights_ref, rest_ref, out_ref):
    rest = rest_ref[...].astype(F32)
    for m in range(base_ref.shape[0]):
        out_ref[m] = weighted(base_ref[m], weights_ref[m], rest, sizes, m, 1, sizes[0] - 1).astype(
            BF16
        )


def own_or_rest(own, rest):
    return jnp.where(lax.axis_index("tp") == 0, own, rest)


def choose_kernel(own_ref, rest_ref, out_ref):
    out_ref[...] = own_or_rest(own_ref[...].astype(F32), rest_ref[...].astype(F32)).astype(BF16)


def pack_kernel(*refs):
    refs[-1][...] = jnp.concatenate([ref[...].astype(F32) for ref in refs[:-1]], 0).astype(BF16)


def shared_expert_kernel(
    mine_ref, other_ref, gate_ref, up_ref, down_ref, keep_ref, send_ref
):
    count = mine_ref.shape[0]
    rows = jnp.concatenate([mine_ref[...].astype(F32), other_ref[...].astype(F32)], 0).astype(BF16)
    gate_val = jnp.dot(rows, gate_ref[...], preferred_element_type=F32)
    up_val = jnp.dot(rows, up_ref[...], preferred_element_type=F32)
    active = (gate_val / (1.0 + jnp.exp(-gate_val)) * up_val).astype(BF16)
    partial_value = jnp.dot(active, down_ref[...], preferred_element_type=F32)
    keep_ref[...] = partial_value[:count]
    send_ref[...] = partial_value[count:].astype(BF16)


def split_members_kernel(keep_ref, got_ref, *out_refs):
    total = keep_ref[...] + got_ref[...].astype(F32)
    count = out_refs[0].shape[0]
    for k, ref in enumerate(out_refs):
        ref[...] = total[k * count : (k + 1) * count].astype(ref.dtype)


def gather_members_kernel(*refs):
    total = refs[0][...]
    for ref in refs[1:-2]:
        total = total + ref[...].astype(F32)
    refs[-2][...] = total
    refs[-1][...] = total.astype(BF16)


def halves_kernel(own_ref, rest_ref, keep_ref, send_ref):
    core = lax.axis_index("tp")
    half = keep_ref.shape[1]

    def columns(which):
        block = pl.ds(pl.multiple_of(which * half, 128), half)
        return own_or_rest(own_ref[:, block], rest_ref[:, block].astype(F32))

    keep_ref[...] = columns(core)
    send_ref[...] = columns(1 - core).astype(BF16)


def kind_weights(table_ref, micro_batch, other, count):
    table = table_ref[micro_batch]
    own, rest = table[:, :count], table[:, count:]
    return own_or_rest(rest, own) if other else own_or_rest(own, rest)


def mine_kernel(sizes, hidden_ref, table_ref, mine_ref, out_ref):
    mine = mine_ref[...]
    count, half = mine.shape
    columns = pl.ds(pl.multiple_of(lax.axis_index("tp") * half, 128), half)
    for m in range(hidden_ref.shape[0]):
        base = hidden_ref[m, :, columns].astype(F32)
        out_ref[m] = weighted(base, kind_weights(table_ref, m, False, count), mine, sizes, m, 0, 1)


def other_kernel(sizes, base_ref, table_ref, other_ref, out_ref):
    other = other_ref[...].astype(F32)
    for m in range(base_ref.shape[0]):
        weights = kind_weights(table_ref, m, True, other.shape[0])
        out_ref[m] = weighted(base_ref[m], weights, other, sizes, m, 0, 1).astype(BF16)


def per_device(hidden, norm_gain, expert_ids, shares, slot_index, w_gate, w_up, w_down):
    micro_count, row_count, model_width = hidden.shape
    top_count = expert_ids.shape[2]
    ep_count = lax.axis_size("ep")
    share_count = lax.axis_size("tp")
    node_size = FF // SLICE // share_count
    nodes = ep_count // node_size
    capacity = row_count * top_count // nodes
    half = model_width // share_count
    per_node = micro_count * capacity
    all_rows = nodes * per_node
    rest_rows = all_rows - per_node
    sizes = (nodes, capacity, per_node)
    ids, placed, weights = (jnp.swapaxes(a, 1, 2) for a in (expert_ids, slot_index, shares))
    small = all_rows <= 32
    params = pltpu.CompilerParams(vmem_limit_bytes=(16 if small else 56) * 1024 * 1024)

    def call(kernel, outs, *args, scratch=(), cost=0):
        return pl.pallas_call(
            kernel,
            out_shape=[jax.ShapeDtypeStruct(shape, kind) for shape, kind in outs],
            scratch_shapes=scratch,
            compiler_params=params,
            cost_estimate=pl.CostEstimate(flops=cost, bytes_accessed=cost // 500, transcendentals=0),
        )(*args)

    def to_member(array, k):
        pairs = [(j, j // node_size * node_size + (j % node_size ^ k)) for j in range(ep_count)]
        return lax.ppermute(array, "ep", pairs)

    def to_nodes(array, sign):
        blocks = []
        for n in range(1, nodes):
            block = array if nodes == 2 else array[(n - 1) * per_node : n * per_node]
            pairs = [(j, (j + sign * n * node_size) % ep_count) for j in range(ep_count)]
            blocks.append(lax.ppermute(block, "ep", pairs))
        return blocks[0] if nodes == 2 else jnp.concatenate(blocks, 0)

    (slot,) = call(slots_kernel, [((all_rows, row_count), jnp.int32)], cost=5 * 10**9)
    own, rest = call(
        functools.partial(dispatch_kernel, sizes, node_size),
        [((per_node, model_width), BF16), ((rest_rows, model_width), BF16)],
        slot,
        hidden,
        norm_gain,
        ids,
        placed,
        cost=20 * 10**9,
    )
    (table,) = call(
        functools.partial(table_kernel, sizes, node_size),
        [((micro_count, row_count, all_rows), F32)],
        slot,
        ids,
        placed,
        weights,
    )
    members = range(1, node_size)
    rows = (micro_count, row_count, half)
    swap = [(i, (i + 1) % share_count) for i in range(share_count)]
    if nodes == 2 and share_count == 2:
        full = (per_node, model_width)

        def to_other_node(array):
            pairs = [(2 * j + 1, 2 * ((j + node_size) % ep_count) + 1) for j in range(ep_count)]
            return lax.ppermute(array, ("ep", "tp"), pairs)

        inbox = to_other_node(rest)
        (mine,) = call(choose_kernel, [(full, BF16)], own, inbox)
        pieces = [mine] + [to_member(mine, k) for k in members]
        packed_shape = (node_size * per_node, model_width)
        (packed,) = call(pack_kernel, [(packed_shape, BF16)], *pieces)
        other = lax.ppermute(packed, "tp", swap)
        keep, send = call(
            shared_expert_kernel,
            [(packed_shape, F32), (packed_shape, BF16)],
            packed,
            other,
            w_gate,
            w_up,
            w_down,
        )
        got = lax.ppermute(send, "tp", swap)
        sums = call(
            split_members_kernel,
            [(full, F32)] + [(full, BF16)] * (node_size - 1),
            keep,
            got,
        )
        arrived = [to_member(sums[k], k) for k in members]
        total, outbox = call(gather_members_kernel, [(full, F32), (full, BF16)], sums[0], *arrived)
        returned = to_other_node(outbox)
        narrow = (per_node, half)
        keep, send = call(halves_kernel, [(narrow, F32), (narrow, BF16)], total, returned)
        other = lax.ppermute(send, "tp", swap)
        (base,) = call(functools.partial(mine_kernel, sizes), [(rows, F32)], hidden, table, keep)
        (mixed,) = call(functools.partial(other_kernel, sizes), [(rows, BF16)], base, table, other)
        return mixed

    inbox = to_nodes(rest, 1)
    owns = [own] + [to_member(own, k) for k in members]
    rests = [inbox] + [to_member(inbox, k) for k in members]
    blocks = (node_size, all_rows, half)
    keep, send = call(
        expert_kernel,
        [(blocks, F32), (blocks, BF16)],
        *[piece for pair in zip(owns, rests) for piece in pair],
        w_gate,
        w_up,
        w_down,
        cost=10**6,
    )
    got = lax.ppermute(send, "tp", swap)
    sums = call(
        add_cores_kernel,
        [
            ((count, half), kind)
            for kind in [F32] + [BF16] * (node_size - 1)
            for count in (per_node, rest_rows)
        ],
        keep,
        got,
    )
    away = [sums[1]] + [to_member(sums[2 * k + 1], k) for k in members]
    home = [sums[0]] + [to_member(sums[2 * k], k) for k in members]
    (outbox,) = call(add_members_kernel, [((rest_rows, half), BF16)], *away)
    returned = to_nodes(outbox, -1)
    (base,) = call(functools.partial(own_kernel, sizes), [(rows, F32)], hidden, table, *home)
    (mixed,) = call(functools.partial(rest_kernel, sizes), [(rows, BF16)], base, table, returned)
    return mixed


def solution(mesh):
    in_specs = (
        P(None, ("groups", "ep"), None),
        P(),
        P(None, ("groups", "ep"), None),
        P(None, ("groups", "ep"), None),
        P(None, ("groups", "ep"), None),
        P(None, ("ep", "tp")),
        P(None, ("ep", "tp")),
        P(("ep", "tp"), None),
    )
    out_specs = P(None, ("groups", "ep"), "tp")
    return jax.shard_map(
        per_device, mesh=mesh, in_specs=in_specs, out_specs=out_specs, check_vma=False
    )
```

```python
import functools

import jax
import jax.numpy as jnp
from jax import lax
from jax.experimental import pallas as pl
from jax.experimental.pallas import tpu as pltpu
from jax.sharding import PartitionSpec as P

FF = 1024
SLICE = 128
BF16 = jnp.bfloat16
F32 = jnp.float32


def hits(ids, placed, slot, sizes, node, micro_batch):
    nodes, capacity, per_node = sizes
    offset = ids - node
    offset = jnp.where(offset < 0, offset + nodes, offset)
    place = jnp.where(placed >= 0, offset * per_node + micro_batch * capacity + placed, -1)
    return [slot == place[k : k + 1, :] for k in range(ids.shape[0])]


def slots_kernel(slot_ref):
    slot_ref[...] = lax.broadcasted_iota(jnp.int32, slot_ref.shape, 0)


def dispatch_kernel(
    sizes, node_size, slot_ref, hidden_ref, gain_ref, ids_ref, placed_ref, own_ref, rest_ref
):
    node = lax.axis_index("ep") // node_size
    gain = gain_ref[...].astype(F32).reshape(1, -1)
    slots = 0.0
    for m in range(hidden_ref.shape[0]):
        flags = hits(ids_ref[m], placed_ref[m], slot_ref[...], sizes, node, m)
        picks = jnp.where(functools.reduce(jnp.logical_or, flags), 1.0, 0.0).astype(BF16)
        values = hidden_ref[m].astype(F32)
        scale = lax.rsqrt(jnp.mean(values * values, axis=-1, keepdims=True) + 1e-06)
        normed = (values * scale * gain).astype(BF16)
        slots = slots + jnp.dot(picks, normed, preferred_element_type=F32)
    per_node = own_ref.shape[0]
    own_ref[...] = slots[:per_node].astype(BF16)
    rest_ref[...] = slots[per_node:].astype(BF16)


def table_kernel(sizes, node_size, slot_ref, ids_ref, placed_ref, shares_ref, table_ref):
    node = lax.axis_index("ep") // node_size
    for m in range(ids_ref.shape[0]):
        flags = hits(ids_ref[m], placed_ref[m], slot_ref[...], sizes, node, m)
        table = sum(
            jnp.where(flag, shares_ref[m][k : k + 1, :], 0.0) for k, flag in enumerate(flags)
        )
        table_ref[m] = table.T


def join_kernel(own_ref, rest_ref, out_ref):
    out_ref[...] = jnp.concatenate([own_ref[...].astype(F32), rest_ref[...].astype(F32)], 0).astype(
        BF16
    )


def hidden_units(pieces, gate_ref, up_ref):
    rows = jnp.concatenate([ref[...].astype(F32) for ref in pieces], 0).astype(BF16)
    gate_val = jnp.dot(rows, gate_ref[...], preferred_element_type=F32)
    up_val = jnp.dot(rows, up_ref[...], preferred_element_type=F32)
    return gate_val / (1.0 + jnp.exp(-gate_val)) * up_val


def early_kernel(*refs):
    refs[-1][...] = hidden_units(refs[:-3], *refs[-3:-1])


def expert_kernel(*refs):
    pieces, (gate_ref, up_ref, early_ref, down_ref, keep_ref, send_ref) = refs[:-6], refs[-6:]
    core = lax.axis_index("tp")
    half = keep_ref.shape[1]
    late = hidden_units(pieces, gate_ref, up_ref)
    active = jnp.concatenate([early_ref[...], late], 0).astype(BF16)

    def down(which):
        columns = pl.ds(pl.multiple_of(which * half, 128), half)
        return jnp.dot(active, down_ref[:, columns], preferred_element_type=F32)

    send_ref[...] = down(1 - core).astype(BF16)
    keep_ref[...] = down(core)


def add_cores_kernel(keep_ref, got_ref, *out_refs):
    total = keep_ref[...] + got_ref[...].astype(F32)
    start = 0
    for ref in out_refs:
        ref[...] = total[start : start + ref.shape[0]].astype(ref.dtype)
        start += ref.shape[0]


def add_members_kernel(*refs):
    count = refs[-1].shape[0]
    total = refs[0][...]
    for ref in refs[1:-1]:
        block = ref[...].astype(F32)
        total = total + block[block.shape[0] - count :]
    refs[-1][...] = total.astype(BF16)


def weighted(base, weights, block, sizes, micro_batch, first, count):
    nodes, capacity, per_node = sizes
    for n in range(count):
        for c in range(capacity):
            slot = n * per_node + micro_batch * capacity + c
            column = first * per_node + slot
            base = base + weights[:, column : column + 1] * block[slot : slot + 1, :]
    return base


def own_kernel(sizes, hidden_ref, weights_ref, *refs):
    own_refs, out_ref = refs[:-1], refs[-1]
    own = own_refs[0][...]
    for ref in own_refs[1:]:
        own = own + ref[...].astype(F32)[: own.shape[0]]
    half = out_ref.shape[2]
    columns = pl.ds(pl.multiple_of(lax.axis_index("tp") * half, 128), half)
    for m in range(hidden_ref.shape[0]):
        base = hidden_ref[m, :, columns].astype(F32)
        out_ref[m] = weighted(base, weights_ref[m], own, sizes, m, 0, 1)


def rest_kernel(sizes, base_ref, weights_ref, rest_ref, out_ref):
    rest = rest_ref[...].astype(F32)
    for m in range(base_ref.shape[0]):
        out_ref[m] = weighted(base_ref[m], weights_ref[m], rest, sizes, m, 1, sizes[0] - 1).astype(
            BF16
        )


def per_device(hidden, norm_gain, expert_ids, shares, slot_index, w_gate, w_up, w_down):
    micro_count, row_count, model_width = hidden.shape
    top_count = expert_ids.shape[2]
    ep_count = lax.axis_size("ep")
    share_count = lax.axis_size("tp")
    node_size = FF // SLICE // share_count
    nodes = ep_count // node_size
    capacity = row_count * top_count // nodes
    half = model_width // share_count
    per_node = micro_count * capacity
    all_rows = nodes * per_node
    rest_rows = all_rows - per_node
    sizes = (nodes, capacity, per_node)
    ids, placed, weights = (jnp.swapaxes(a, 1, 2) for a in (expert_ids, slot_index, shares))
    small = all_rows <= 32
    params = pltpu.CompilerParams(vmem_limit_bytes=(16 if small else 56) * 1024 * 1024)

    def call(kernel, outs, *args, scratch=(), cost=0):
        return pl.pallas_call(
            kernel,
            out_shape=[jax.ShapeDtypeStruct(shape, kind) for shape, kind in outs],
            scratch_shapes=scratch,
            compiler_params=params,
            cost_estimate=pl.CostEstimate(flops=cost, bytes_accessed=cost // 500, transcendentals=0),
        )(*args)

    def to_member(array, k):
        pairs = [(j, j // node_size * node_size + (j % node_size ^ k)) for j in range(ep_count)]
        return lax.ppermute(array, "ep", pairs)

    def to_nodes(array, sign):
        blocks = []
        for n in range(1, nodes):
            block = array if nodes == 2 else array[(n - 1) * per_node : n * per_node]
            pairs = [(j, (j + sign * n * node_size) % ep_count) for j in range(ep_count)]
            blocks.append(lax.ppermute(block, "ep", pairs))
        return blocks[0] if nodes == 2 else jnp.concatenate(blocks, 0)

    (slot,) = call(slots_kernel, [((all_rows, row_count), jnp.int32)], cost=5 * 10**9)
    own, rest = call(
        functools.partial(dispatch_kernel, sizes, node_size),
        [((per_node, model_width), BF16), ((rest_rows, model_width), BF16)],
        slot,
        hidden,
        norm_gain,
        ids,
        placed,
        cost=20 * 10**9,
    )
    (table,) = call(
        functools.partial(table_kernel, sizes, node_size),
        [((micro_count, row_count, all_rows), F32)],
        slot,
        ids,
        placed,
        weights,
    )
    inbox = to_nodes(rest, 1)
    own_one, own_two = to_member(own, 1), to_member(own, 2)
    (joined,) = call(join_kernel, [((all_rows, model_width), BF16)], own, inbox)
    far = to_member(joined, 3)
    rest_two, rest_one = to_member(inbox, 2), to_member(inbox, 1)
    (early,) = call(
        early_kernel,
        [((3 * per_node, w_gate.shape[1]), F32)],
        own,
        own_one,
        own_two,
        w_gate,
        w_up,
        cost=4 * 10**9,
    )
    block = (node_size * all_rows, half)
    keep, send = call(
        expert_kernel,
        [(block, F32), (block, BF16)],
        inbox,
        rest_one,
        rest_two,
        far,
        w_gate,
        w_up,
        early,
        w_down,
        cost=10**6,
    )
    got = lax.ppermute(send, "tp", [(i, (i + 1) % share_count) for i in range(share_count)])
    narrow, wide = (per_node, half), (rest_rows, half)
    own, own_one, own_two, rest, rest_one, rest_two, own_far, rest_far = call(
        add_cores_kernel,
        [(narrow, F32)]
        + [(narrow, BF16)] * 2
        + [(wide, F32)]
        + [(wide, BF16)] * 2
        + [(narrow, BF16), (wide, BF16)],
        keep,
        got,
    )
    rest_far, rest_two = to_member(rest_far, 3), to_member(rest_two, 2)
    (near,) = call(join_kernel, [((all_rows, half), BF16)], own_one, rest_one)
    near = to_member(near, 1)
    own_far, own_two = to_member(own_far, 3), to_member(own_two, 2)
    home = [own, near, own_far, own_two]
    (outbox,) = call(add_members_kernel, [(wide, BF16)], rest, rest_far, rest_two, near)
    returned = to_nodes(outbox, -1)
    rows = (micro_count, row_count, half)
    (base,) = call(functools.partial(own_kernel, sizes), [(rows, F32)], hidden, table, *home)
    (mixed,) = call(functools.partial(rest_kernel, sizes), [(rows, BF16)], base, table, returned)
    return mixed


def solution(mesh):
    in_specs = (
        P(None, ("groups", "ep"), None),
        P(),
        P(None, ("groups", "ep"), None),
        P(None, ("groups", "ep"), None),
        P(None, ("groups", "ep"), None),
        P(None, ("ep", "tp")),
        P(None, ("ep", "tp")),
        P(("ep", "tp"), None),
    )
    out_specs = P(None, ("groups", "ep"), "tp")
    return jax.shard_map(
        per_device, mesh=mesh, in_specs=in_specs, out_specs=out_specs, check_vma=False
    )
```

```python
import functools

import jax
import jax.numpy as jnp
from jax import lax
from jax.experimental import pallas as pl
from jax.experimental.pallas import tpu as pltpu
from jax.sharding import PartitionSpec as P

FF = 1024
SLICE = 128
BF16 = jnp.bfloat16
F32 = jnp.float32


def hits(ids, placed, slot, sizes, node, micro_batch):
    nodes, capacity, per_node = sizes
    offset = ids - node
    offset = jnp.where(offset < 0, offset + nodes, offset)
    place = jnp.where(placed >= 0, offset * per_node + micro_batch * capacity + placed, -1)
    return [slot == place[k : k + 1, :] for k in range(ids.shape[0])]


def slots_kernel(slot_ref):
    slot_ref[...] = lax.broadcasted_iota(jnp.int32, slot_ref.shape, 0)


def dispatch_kernel(
    sizes, node_size, slot_ref, hidden_ref, gain_ref, ids_ref, placed_ref, own_ref, rest_ref
):
    node = lax.axis_index("ep") // node_size
    gain = gain_ref[...].astype(F32).reshape(1, -1)
    slots = 0.0
    for m in range(hidden_ref.shape[0]):
        flags = hits(ids_ref[m], placed_ref[m], slot_ref[...], sizes, node, m)
        picks = jnp.where(functools.reduce(jnp.logical_or, flags), 1.0, 0.0).astype(BF16)
        values = hidden_ref[m].astype(F32)
        scale = lax.rsqrt(jnp.mean(values * values, axis=-1, keepdims=True) + 1e-06)
        normed = (values * scale * gain).astype(BF16)
        slots = slots + jnp.dot(picks, normed, preferred_element_type=F32)
    per_node = own_ref.shape[0]
    own_ref[...] = slots[:per_node].astype(BF16)
    rest_ref[...] = slots[per_node:].astype(BF16)


def table_kernel(sizes, node_size, slot_ref, ids_ref, placed_ref, shares_ref, table_ref):
    node = lax.axis_index("ep") // node_size
    for m in range(ids_ref.shape[0]):
        flags = hits(ids_ref[m], placed_ref[m], slot_ref[...], sizes, node, m)
        table = sum(
            jnp.where(flag, shares_ref[m][k : k + 1, :], 0.0) for k, flag in enumerate(flags)
        )
        table_ref[m] = table.T


def join_kernel(own_ref, rest_ref, out_ref):
    out_ref[...] = jnp.concatenate([own_ref[...].astype(F32), rest_ref[...].astype(F32)], 0).astype(
        BF16
    )


def hidden_units(pieces, gate_ref, up_ref):
    rows = jnp.concatenate([ref[...].astype(F32) for ref in pieces], 0).astype(BF16)
    gate_val = jnp.dot(rows, gate_ref[...], preferred_element_type=F32)
    up_val = jnp.dot(rows, up_ref[...], preferred_element_type=F32)
    return gate_val / (1.0 + jnp.exp(-gate_val)) * up_val


def early_kernel(*refs):
    refs[-1][...] = hidden_units(refs[:-3], *refs[-3:-1])


def down_halves(active, down_ref, keep_ref, send_ref):
    core = lax.axis_index("tp")
    half = keep_ref.shape[1]

    def down(which):
        columns = pl.ds(pl.multiple_of(which * half, 128), half)
        return jnp.dot(active, down_ref[:, columns], preferred_element_type=F32)

    send_ref[...] = down(1 - core).astype(BF16)
    keep_ref[...] = down(core)


def expert_kernel(*refs):
    pieces, (gate_ref, up_ref, early_ref, down_ref, keep_ref, send_ref) = refs[:-6], refs[-6:]
    late = hidden_units(pieces, gate_ref, up_ref)
    active = jnp.concatenate([early_ref[...], late], 0).astype(BF16)
    down_halves(active, down_ref, keep_ref, send_ref)


def pack_kernel(hop_ref, pass_ref, side_ref, unread_ref, out_ref):
    out_ref[...] = jnp.concatenate(
        [ref[...].astype(F32) for ref in (hop_ref, pass_ref, side_ref)], 0
    ).astype(BF16)


def shared_expert_kernel(
    count,
    hop_ref,
    pass_ref,
    other_ref,
    gate_ref,
    up_ref,
    early_ref,
    down_ref,
    keep_ref,
    keep_own_ref,
    send_ref,
    own_ref,
):
    core = lax.axis_index("tp")
    half = keep_own_ref.shape[1]
    late = hidden_units((hop_ref, pass_ref, other_ref), gate_ref, up_ref)
    early = early_ref[...]
    active = jnp.concatenate([late[: 2 * count], early[2 * count :], late[2 * count :]], 0)
    active = jnp.concatenate([active, early[: 2 * count]], 0).astype(BF16)
    product = jnp.dot(active, down_ref[...], preferred_element_type=F32)
    keep_ref[...] = product[: 3 * count]
    own_ref[...] = product[6 * count :]
    keep_own_ref[...] = own_ref[:, pl.ds(pl.multiple_of(core * half, 128), half)]
    own = own_ref[:, pl.ds(pl.multiple_of((1 - core) * half, 128), half)]
    send = product[3 * count : 6 * count]
    send_ref[...] = jnp.concatenate([send[:, :half], send[:, half:], own], 0).astype(BF16)


def shared_sums_kernel(
    keep_ref, keep_own_ref, got_ref, hop_ref, pass_ref, side_ref, own_ref, two_ref
):
    count, half = own_ref.shape
    got = got_ref[...].astype(F32)
    total = keep_ref[...] + jnp.concatenate([got[: 3 * count], got[3 * count : 6 * count]], 1)
    hop_ref[...] = total[:count]
    pass_ref[...] = total[count : 2 * count].astype(BF16)
    side_ref[...] = total[2 * count :].astype(BF16)
    own = keep_own_ref[...] + got[6 * count :]
    own_ref[...] = own[:count]
    two_ref[...] = own[count:]


def halves_kernel(own_ref, two_ref, side_ref, back_ref, own_out, back_out, send_ref):
    core = lax.axis_index("tp")
    half = back_out.shape[1]
    mine = pl.ds(pl.multiple_of(core * half, 128), half)
    other = pl.ds(pl.multiple_of((1 - core) * half, 128), half)
    own_out[...] = own_ref[...] + two_ref[...] + side_ref[:, mine].astype(F32)
    back_out[...] = back_ref[:, mine]
    send_ref[...] = jnp.concatenate(
        [side_ref[:, other].astype(F32), back_ref[:, other].astype(F32)], 0
    ).astype(BF16)


def base_kernel(sizes, hidden_ref, table_ref, own_ref, back_ref, out_ref):
    own = own_ref[...]
    back = back_ref[...].astype(F32)
    half = out_ref.shape[2]
    columns = pl.ds(pl.multiple_of(lax.axis_index("tp") * half, 128), half)
    for m in range(hidden_ref.shape[0]):
        base = hidden_ref[m, :, columns].astype(F32)
        base = weighted(base, table_ref[m], own, sizes, m, 0, 1)
        out_ref[m] = weighted(base, table_ref[m], back, sizes, m, 1, 1)


def last_kernel(sizes, base_ref, table_ref, got_ref, out_ref):
    got = got_ref[...].astype(F32)
    count = got.shape[0] // 2
    for m in range(base_ref.shape[0]):
        base = weighted(base_ref[m], table_ref[m], got[:count], sizes, m, 0, 1)
        out_ref[m] = weighted(base, table_ref[m], got[count:], sizes, m, 1, 1).astype(BF16)


def add_cores_kernel(keep_ref, got_ref, *out_refs):
    total = keep_ref[...] + got_ref[...].astype(F32)
    start = 0
    for ref in out_refs:
        ref[...] = total[start : start + ref.shape[0]].astype(ref.dtype)
        start += ref.shape[0]


def add_members_kernel(*refs):
    count = refs[-1].shape[0]
    total = refs[0][...]
    for ref in refs[1:-1]:
        block = ref[...].astype(F32)
        total = total + block[block.shape[0] - count :]
    refs[-1][...] = total.astype(BF16)


def weighted(base, weights, block, sizes, micro_batch, first, count):
    nodes, capacity, per_node = sizes
    for n in range(count):
        for c in range(capacity):
            slot = n * per_node + micro_batch * capacity + c
            column = first * per_node + slot
            base = base + weights[:, column : column + 1] * block[slot : slot + 1, :]
    return base


def own_kernel(sizes, hidden_ref, weights_ref, *refs):
    own_refs, out_ref = refs[:-1], refs[-1]
    own = own_refs[0][...]
    for ref in own_refs[1:]:
        own = own + ref[...].astype(F32)[: own.shape[0]]
    half = out_ref.shape[2]
    columns = pl.ds(pl.multiple_of(lax.axis_index("tp") * half, 128), half)
    for m in range(hidden_ref.shape[0]):
        base = hidden_ref[m, :, columns].astype(F32)
        out_ref[m] = weighted(base, weights_ref[m], own, sizes, m, 0, 1)


def rest_kernel(sizes, base_ref, weights_ref, rest_ref, out_ref):
    rest = rest_ref[...].astype(F32)
    for m in range(base_ref.shape[0]):
        out_ref[m] = weighted(base_ref[m], weights_ref[m], rest, sizes, m, 1, sizes[0] - 1).astype(
            BF16
        )


def per_device(hidden, norm_gain, expert_ids, shares, slot_index, w_gate, w_up, w_down):
    micro_count, row_count, model_width = hidden.shape
    top_count = expert_ids.shape[2]
    ep_count = lax.axis_size("ep")
    share_count = lax.axis_size("tp")
    node_size = FF // SLICE // share_count
    nodes = ep_count // node_size
    capacity = row_count * top_count // nodes
    half = model_width // share_count
    per_node = micro_count * capacity
    all_rows = nodes * per_node
    rest_rows = all_rows - per_node
    sizes = (nodes, capacity, per_node)
    ids, placed, weights = (jnp.swapaxes(a, 1, 2) for a in (expert_ids, slot_index, shares))
    small = all_rows <= 32
    params = pltpu.CompilerParams(vmem_limit_bytes=(16 if small else 56) * 1024 * 1024)

    def call(kernel, outs, *args, scratch=(), cost=0):
        return pl.pallas_call(
            kernel,
            out_shape=[jax.ShapeDtypeStruct(shape, kind) for shape, kind in outs],
            scratch_shapes=scratch,
            compiler_params=params,
            cost_estimate=pl.CostEstimate(flops=cost, bytes_accessed=cost // 500, transcendentals=0),
        )(*args)

    def to_member(array, k):
        pairs = [(j, j // node_size * node_size + (j % node_size ^ k)) for j in range(ep_count)]
        return lax.ppermute(array, "ep", pairs)

    def to_nodes(array, sign):
        blocks = []
        for n in range(1, nodes):
            block = array if nodes == 2 else array[(n - 1) * per_node : n * per_node]
            pairs = [(j, (j + sign * n * node_size) % ep_count) for j in range(ep_count)]
            blocks.append(lax.ppermute(block, "ep", pairs))
        return blocks[0] if nodes == 2 else jnp.concatenate(blocks, 0)

    (slot,) = call(slots_kernel, [((all_rows, row_count), jnp.int32)], cost=5 * 10**9)
    own, rest = call(
        functools.partial(dispatch_kernel, sizes, node_size),
        [((per_node, model_width), BF16), ((rest_rows, model_width), BF16)],
        slot,
        hidden,
        norm_gain,
        ids,
        placed,
        cost=20 * 10**9,
    )
    (table,) = call(
        functools.partial(table_kernel, sizes, node_size),
        [((micro_count, row_count, all_rows), F32)],
        slot,
        ids,
        placed,
        weights,
    )
    block = (node_size * all_rows, half)
    hidden_block = ((3 * per_node, w_gate.shape[1]), F32)

    def early_rows(*pieces):
        (early,) = call(early_kernel, [hidden_block], *pieces, w_gate, w_up, cost=4 * 10**9)
        return early

    if nodes == 2 and node_size == 4 and share_count == 2:

        def by_core(array, flip_zero, flip_one):
            pairs = []
            for j in range(ep_count):
                pairs += [(2 * j, 2 * (j ^ flip_zero)), (2 * j + 1, 2 * (j ^ flip_one) + 1)]
            return lax.ppermute(array, ("ep", "tp"), pairs)

        swap = [(0, 1), (1, 0)]
        full, narrow = (per_node, model_width), (per_node, half)
        hop = by_core(rest, node_size, node_size ^ 2)
        own_two, own_side = to_member(own, 2), by_core(own, 1, 3)
        passed = to_member(hop, 1)
        early = early_rows(own, own_two, own_side)
        (packed,) = call(pack_kernel, [((3 * per_node, model_width), BF16)], hop, passed, own_side, own_two)
        other = lax.ppermute(packed, "tp", swap)
        keep, keep_own, send = call(
            functools.partial(shared_expert_kernel, per_node),
            [
                ((3 * per_node, model_width), F32),
                ((2 * per_node, half), F32),
                ((8 * per_node, half), BF16),
            ],
            hop,
            passed,
            other,
            w_gate,
            w_up,
            early,
            w_down,
            scratch=[pltpu.VMEM((2 * per_node, model_width), F32)],
            cost=10**6,
        )
        got = lax.ppermute(send, "tp", swap)
        hop, passed, side, own, two = call(
            shared_sums_kernel,
            [(full, F32), (full, BF16), (full, BF16), (narrow, F32), (narrow, F32)],
            keep,
            keep_own,
            got,
        )
        passed = to_member(passed, 1)
        side, two = by_core(side, 1, 3), to_member(two, 2)
        (outbox,) = call(add_members_kernel, [(full, BF16)], hop, passed)
        back = by_core(outbox, node_size, node_size ^ 2)
        own, back, send = call(
            halves_kernel,
            [(narrow, F32), (narrow, BF16), ((2 * per_node, half), BF16)],
            own,
            two,
            side,
            back,
        )
        got = lax.ppermute(send, "tp", swap)
        rows = (micro_count, row_count, half)
        (base,) = call(
            functools.partial(base_kernel, sizes),
            [(rows, F32)],
            hidden,
            table,
            own,
            back,
        )
        (mixed,) = call(functools.partial(last_kernel, sizes), [(rows, BF16)], base, table, got)
        return mixed

    names = ("own", "own_one", "own_two", "rest", "rest_one", "rest_two", "own_far", "rest_far")
    inbox = to_nodes(rest, 1)
    own_one, own_two = to_member(own, 1), to_member(own, 2)
    (joined,) = call(join_kernel, [((all_rows, model_width), BF16)], own, inbox)
    far = to_member(joined, 3)
    rest_two, rest_one = to_member(inbox, 2), to_member(inbox, 1)
    early = early_rows(own, own_one, own_two)
    keep, send = call(
        expert_kernel,
        [(block, F32), (block, BF16)],
        inbox,
        rest_one,
        rest_two,
        far,
        w_gate,
        w_up,
        early,
        w_down,
        cost=10**6,
    )
    got = lax.ppermute(send, "tp", [(i, (i + 1) % share_count) for i in range(share_count)])
    narrow, wide = (per_node, half), (rest_rows, half)
    shapes = [
        (narrow if name.startswith("own") else wide, F32 if name in ("own", "rest") else BF16)
        for name in names
    ]
    sums = dict(zip(names, call(add_cores_kernel, shapes, keep, got)))
    own, own_one, own_two, own_far = (sums[n] for n in ("own", "own_one", "own_two", "own_far"))
    rest, rest_one, rest_two, rest_far = (
        sums[n] for n in ("rest", "rest_one", "rest_two", "rest_far")
    )
    rest_far, rest_two = to_member(rest_far, 3), to_member(rest_two, 2)
    (near,) = call(join_kernel, [((all_rows, half), BF16)], own_one, rest_one)
    near = to_member(near, 1)
    own_far, own_two = to_member(own_far, 3), to_member(own_two, 2)
    home = [own, near, own_far, own_two]
    (outbox,) = call(add_members_kernel, [(wide, BF16)], rest, rest_far, rest_two, near)
    returned = to_nodes(outbox, -1)
    rows = (micro_count, row_count, half)
    (base,) = call(functools.partial(own_kernel, sizes), [(rows, F32)], hidden, table, *home)
    (mixed,) = call(functools.partial(rest_kernel, sizes), [(rows, BF16)], base, table, returned)
    return mixed


def solution(mesh):
    in_specs = (
        P(None, ("groups", "ep"), None),
        P(),
        P(None, ("groups", "ep"), None),
        P(None, ("groups", "ep"), None),
        P(None, ("groups", "ep"), None),
        P(None, ("ep", "tp")),
        P(None, ("ep", "tp")),
        P(("ep", "tp"), None),
    )
    out_specs = P(None, ("groups", "ep"), "tp")
    return jax.shard_map(
        per_device, mesh=mesh, in_specs=in_specs, out_specs=out_specs, check_vma=False
    )
```

```python
import functools

import jax
import jax.numpy as jnp
from jax import lax
from jax.experimental import pallas as pl
from jax.experimental.pallas import tpu as pltpu
from jax.sharding import PartitionSpec as P

FF = 1024
SLICE = 128
BF16 = jnp.bfloat16
F32 = jnp.float32


def hits(ids, placed, slot, sizes, node, micro_batch):
    nodes, capacity, per_node = sizes
    offset = ids - node
    offset = jnp.where(offset < 0, offset + nodes, offset)
    place = jnp.where(placed >= 0, offset * per_node + micro_batch * capacity + placed, -1)
    return [slot == place[k : k + 1, :] for k in range(ids.shape[0])]


def slots_kernel(slot_ref):
    slot_ref[...] = lax.broadcasted_iota(jnp.int32, slot_ref.shape, 0)


def dispatch_kernel(
    sizes, node_size, slot_ref, hidden_ref, gain_ref, ids_ref, placed_ref, own_ref, rest_ref
):
    node = lax.axis_index("ep") // node_size
    gain = gain_ref[...].astype(F32).reshape(1, -1)
    slots = 0.0
    for m in range(hidden_ref.shape[0]):
        flags = hits(ids_ref[m], placed_ref[m], slot_ref[...], sizes, node, m)
        picks = jnp.where(functools.reduce(jnp.logical_or, flags), 1.0, 0.0).astype(BF16)
        values = hidden_ref[m].astype(F32)
        scale = lax.rsqrt(jnp.mean(values * values, axis=-1, keepdims=True) + 1e-06)
        normed = (values * scale * gain).astype(BF16)
        slots = slots + jnp.dot(picks, normed, preferred_element_type=F32)
    per_node = own_ref.shape[0]
    own_ref[...] = slots[:per_node].astype(BF16)
    rest_ref[...] = slots[per_node:].astype(BF16)


def table_kernel(sizes, node_size, slot_ref, ids_ref, placed_ref, shares_ref, table_ref):
    node = lax.axis_index("ep") // node_size
    for m in range(ids_ref.shape[0]):
        flags = hits(ids_ref[m], placed_ref[m], slot_ref[...], sizes, node, m)
        table = sum(
            jnp.where(flag, shares_ref[m][k : k + 1, :], 0.0) for k, flag in enumerate(flags)
        )
        table_ref[m] = table.T


def join_kernel(own_ref, rest_ref, out_ref):
    out_ref[...] = jnp.concatenate([own_ref[...].astype(F32), rest_ref[...].astype(F32)], 0).astype(
        BF16
    )


def hidden_units(pieces, gate_ref, up_ref):
    rows = jnp.concatenate([ref[...].astype(F32) for ref in pieces], 0).astype(BF16)
    gate_val = jnp.dot(rows, gate_ref[...], preferred_element_type=F32)
    up_val = jnp.dot(rows, up_ref[...], preferred_element_type=F32)
    return gate_val / (1.0 + jnp.exp(-gate_val)) * up_val


def early_kernel(*refs):
    refs[-1][...] = hidden_units(refs[:-3], *refs[-3:-1])


def down_halves(active, down_ref, keep_ref, send_ref):
    core = lax.axis_index("tp")
    half = keep_ref.shape[1]

    def down(which):
        columns = pl.ds(pl.multiple_of(which * half, 128), half)
        return jnp.dot(active, down_ref[:, columns], preferred_element_type=F32)

    send_ref[...] = down(1 - core).astype(BF16)
    keep_ref[...] = down(core)


def expert_kernel(*refs):
    pieces, (gate_ref, up_ref, early_ref, down_ref, keep_ref, send_ref) = refs[:-6], refs[-6:]
    late = hidden_units(pieces, gate_ref, up_ref)
    active = jnp.concatenate([early_ref[...], late], 0).astype(BF16)
    down_halves(active, down_ref, keep_ref, send_ref)


def own_or_rest(own, rest):
    return jnp.where(lax.axis_index("tp") == 0, own, rest)


def chip_product(rows, weight_refs):
    total = 0.0
    for gate_ref, up_ref, down_ref in (weight_refs[:3], weight_refs[3:]):
        gate_val = jnp.dot(rows, gate_ref[...], preferred_element_type=F32)
        up_val = jnp.dot(rows, up_ref[...], preferred_element_type=F32)
        active = (gate_val / (1.0 + jnp.exp(-gate_val)) * up_val).astype(BF16)
        total = total + jnp.dot(active, down_ref[...], preferred_element_type=F32)
    return total


def chip_early_kernel(rows_ref, *refs):
    refs[-1][...] = chip_product(rows_ref[...], refs[:6]).astype(BF16)


def chip_late_kernel(early_ref, hop_ref, passed_ref, own_ref, two_ref, *refs):
    weight_refs, (hop_out, passed_out, own_out, two_out) = refs[:6], refs[6:]
    count = hop_ref.shape[0]
    hop, passed, own, two = (
        ref[...].astype(F32) for ref in (hop_ref, passed_ref, own_ref, two_ref)
    )
    rows = jnp.concatenate([hop, passed, own_or_rest(own, two)], 0).astype(BF16)
    total = chip_product(rows, weight_refs)
    hop_out[...] = total[:count]
    passed_out[...] = total[count : 2 * count].astype(BF16)
    own_out[...] = total[2 * count :]
    two_out[...] = total[2 * count :].astype(BF16)


def halves_kernel(own_ref, two_ref, side_ref, back_ref, own_out, back_out, send_ref):
    core = lax.axis_index("tp")
    half = back_out.shape[1]

    def columns(which):
        block = pl.ds(pl.multiple_of(which * half, 128), half)
        own = own_or_rest(own_ref[:, block], two_ref[:, block].astype(F32))
        return own + side_ref[:, block].astype(F32), back_ref[:, block].astype(F32)

    own_out[...], back_out[...] = columns(core)
    send_ref[...] = jnp.concatenate(columns(1 - core), 0).astype(BF16)


def base_kernel(sizes, hidden_ref, table_ref, own_ref, back_ref, out_ref):
    own, back = own_ref[...], back_ref[...]
    half = out_ref.shape[2]
    columns = pl.ds(pl.multiple_of(lax.axis_index("tp") * half, 128), half)
    for m in range(hidden_ref.shape[0]):
        base = hidden_ref[m, :, columns].astype(F32)
        base = weighted(base, table_ref[m], own, sizes, m, 0, 1)
        out_ref[m] = weighted(base, table_ref[m], back, sizes, m, 1, 1)


def last_kernel(sizes, base_ref, table_ref, got_ref, out_ref):
    got = got_ref[...].astype(F32)
    count = got.shape[0] // 2
    for m in range(base_ref.shape[0]):
        base = weighted(base_ref[m], table_ref[m], got[:count], sizes, m, 0, 1)
        out_ref[m] = weighted(base, table_ref[m], got[count:], sizes, m, 1, 1).astype(BF16)


def add_cores_kernel(keep_ref, got_ref, *out_refs):
    total = keep_ref[...] + got_ref[...].astype(F32)
    start = 0
    for ref in out_refs:
        ref[...] = total[start : start + ref.shape[0]].astype(ref.dtype)
        start += ref.shape[0]


def add_members_kernel(*refs):
    count = refs[-1].shape[0]
    total = refs[0][...]
    for ref in refs[1:-1]:
        block = ref[...].astype(F32)
        total = total + block[block.shape[0] - count :]
    refs[-1][...] = total.astype(BF16)


def weighted(base, weights, block, sizes, micro_batch, first, count):
    nodes, capacity, per_node = sizes
    for n in range(count):
        for c in range(capacity):
            slot = n * per_node + micro_batch * capacity + c
            column = first * per_node + slot
            base = base + weights[:, column : column + 1] * block[slot : slot + 1, :]
    return base


def own_kernel(sizes, hidden_ref, weights_ref, *refs):
    own_refs, out_ref = refs[:-1], refs[-1]
    own = own_refs[0][...]
    for ref in own_refs[1:]:
        own = own + ref[...].astype(F32)[: own.shape[0]]
    half = out_ref.shape[2]
    columns = pl.ds(pl.multiple_of(lax.axis_index("tp") * half, 128), half)
    for m in range(hidden_ref.shape[0]):
        base = hidden_ref[m, :, columns].astype(F32)
        out_ref[m] = weighted(base, weights_ref[m], own, sizes, m, 0, 1)


def rest_kernel(sizes, base_ref, weights_ref, rest_ref, out_ref):
    rest = rest_ref[...].astype(F32)
    for m in range(base_ref.shape[0]):
        out_ref[m] = weighted(base_ref[m], weights_ref[m], rest, sizes, m, 1, sizes[0] - 1).astype(
            BF16
        )


def per_device(hidden, norm_gain, expert_ids, shares, slot_index, w_gate, w_up, w_down):
    micro_count, row_count, model_width = hidden.shape
    top_count = expert_ids.shape[2]
    ep_count = lax.axis_size("ep")
    share_count = lax.axis_size("tp")
    node_size = FF // SLICE // share_count
    nodes = ep_count // node_size
    capacity = row_count * top_count // nodes
    half = model_width // share_count
    per_node = micro_count * capacity
    all_rows = nodes * per_node
    rest_rows = all_rows - per_node
    sizes = (nodes, capacity, per_node)
    ids, placed, weights = (jnp.swapaxes(a, 1, 2) for a in (expert_ids, slot_index, shares))
    small = all_rows <= 32
    params = pltpu.CompilerParams(vmem_limit_bytes=(16 if small else 56) * 1024 * 1024)

    def call(kernel, outs, *args, scratch=(), cost=0):
        return pl.pallas_call(
            kernel,
            out_shape=[jax.ShapeDtypeStruct(shape, kind) for shape, kind in outs],
            scratch_shapes=scratch,
            compiler_params=params,
            cost_estimate=pl.CostEstimate(flops=cost, bytes_accessed=cost // 500, transcendentals=0),
        )(*args)

    def to_member(array, k):
        pairs = [(j, j // node_size * node_size + (j % node_size ^ k)) for j in range(ep_count)]
        return lax.ppermute(array, "ep", pairs)

    def to_nodes(array, sign):
        blocks = []
        for n in range(1, nodes):
            block = array if nodes == 2 else array[(n - 1) * per_node : n * per_node]
            pairs = [(j, (j + sign * n * node_size) % ep_count) for j in range(ep_count)]
            blocks.append(lax.ppermute(block, "ep", pairs))
        return blocks[0] if nodes == 2 else jnp.concatenate(blocks, 0)

    (slot,) = call(slots_kernel, [((all_rows, row_count), jnp.int32)], cost=5 * 10**9)
    own, rest = call(
        functools.partial(dispatch_kernel, sizes, node_size),
        [((per_node, model_width), BF16), ((rest_rows, model_width), BF16)],
        slot,
        hidden,
        norm_gain,
        ids,
        placed,
        cost=20 * 10**9,
    )
    (table,) = call(
        functools.partial(table_kernel, sizes, node_size),
        [((micro_count, row_count, all_rows), F32)],
        slot,
        ids,
        placed,
        weights,
    )
    block = (node_size * all_rows, half)

    def early_rows(*pieces):
        shape = (sum(piece.shape[0] for piece in pieces), w_gate.shape[1])
        (early,) = call(early_kernel, [(shape, F32)], *pieces, w_gate, w_up, cost=4 * 10**9)
        return early

    if nodes == 2 and node_size == 4 and share_count == 2:

        def by_core(array, flip_zero, flip_one):
            pairs = []
            for j in range(ep_count):
                pairs += [(2 * j, 2 * (j ^ flip_zero)), (2 * j + 1, 2 * (j ^ flip_one) + 1)]
            return lax.ppermute(array, ("ep", "tp"), pairs)

        swap = [(0, 1), (1, 0)]
        full, narrow = (per_node, model_width), (per_node, half)
        weights = [w_gate, w_up, w_down]
        weights += [lax.ppermute(array, "tp", swap) for array in weights]
        hop = by_core(rest, node_size, node_size ^ 2)
        two, side = to_member(own, 2), by_core(own, 1, 3)
        passed = to_member(hop, 1)
        (side,) = call(chip_early_kernel, [(full, BF16)], side, *weights, cost=4 * 10**9)
        hop, passed, own, two = call(
            chip_late_kernel,
            [(full, F32), (full, BF16), (full, F32), (full, BF16)],
            side,
            hop,
            passed,
            own,
            two,
            *weights,
            cost=10**6,
        )
        passed = to_member(passed, 1)
        side, two = by_core(side, 1, 3), to_member(two, 2)
        (outbox,) = call(add_members_kernel, [(full, BF16)], hop, passed)
        back = by_core(outbox, node_size, node_size ^ 2)
        own, back, send = call(
            halves_kernel,
            [(narrow, F32), (narrow, F32), ((2 * per_node, half), BF16)],
            own,
            two,
            side,
            back,
        )
        got = lax.ppermute(send, "tp", swap)
        rows = (micro_count, row_count, half)
        (base,) = call(
            functools.partial(base_kernel, sizes),
            [(rows, F32)],
            hidden,
            table,
            own,
            back,
        )
        (mixed,) = call(functools.partial(last_kernel, sizes), [(rows, BF16)], base, table, got)
        return mixed

    names = ("own", "own_one", "own_two", "rest", "rest_one", "rest_two", "own_far", "rest_far")
    inbox = to_nodes(rest, 1)
    own_one, own_two = to_member(own, 1), to_member(own, 2)
    (joined,) = call(join_kernel, [((all_rows, model_width), BF16)], own, inbox)
    far = to_member(joined, 3)
    rest_two, rest_one = to_member(inbox, 2), to_member(inbox, 1)
    early = early_rows(own, own_one, own_two)
    keep, send = call(
        expert_kernel,
        [(block, F32), (block, BF16)],
        inbox,
        rest_one,
        rest_two,
        far,
        w_gate,
        w_up,
        early,
        w_down,
        cost=10**6,
    )
    got = lax.ppermute(send, "tp", [(i, (i + 1) % share_count) for i in range(share_count)])
    narrow, wide = (per_node, half), (rest_rows, half)
    shapes = [
        (narrow if name.startswith("own") else wide, F32 if name in ("own", "rest") else BF16)
        for name in names
    ]
    sums = dict(zip(names, call(add_cores_kernel, shapes, keep, got)))
    own, own_one, own_two, own_far = (sums[n] for n in ("own", "own_one", "own_two", "own_far"))
    rest, rest_one, rest_two, rest_far = (
        sums[n] for n in ("rest", "rest_one", "rest_two", "rest_far")
    )
    rest_far, rest_two = to_member(rest_far, 3), to_member(rest_two, 2)
    (near,) = call(join_kernel, [((all_rows, half), BF16)], own_one, rest_one)
    near = to_member(near, 1)
    own_far, own_two = to_member(own_far, 3), to_member(own_two, 2)
    home = [own, near, own_far, own_two]
    (outbox,) = call(add_members_kernel, [(wide, BF16)], rest, rest_far, rest_two, near)
    returned = to_nodes(outbox, -1)
    rows = (micro_count, row_count, half)
    (base,) = call(functools.partial(own_kernel, sizes), [(rows, F32)], hidden, table, *home)
    (mixed,) = call(functools.partial(rest_kernel, sizes), [(rows, BF16)], base, table, returned)
    return mixed


def solution(mesh):
    in_specs = (
        P(None, ("groups", "ep"), None),
        P(),
        P(None, ("groups", "ep"), None),
        P(None, ("groups", "ep"), None),
        P(None, ("groups", "ep"), None),
        P(None, ("ep", "tp")),
        P(None, ("ep", "tp")),
        P(("ep", "tp"), None),
    )
    out_specs = P(None, ("groups", "ep"), "tp")
    return jax.shard_map(
        per_device, mesh=mesh, in_specs=in_specs, out_specs=out_specs, check_vma=False
    )
```

```python
import functools

import jax
import jax.numpy as jnp
from jax import lax
from jax.experimental import pallas as pl
from jax.experimental.pallas import tpu as pltpu
from jax.sharding import PartitionSpec as P

FF = 1024
SLICE = 128
BF16 = jnp.bfloat16
F32 = jnp.float32


def hits(ids, placed, slot, sizes, node, micro_batch):
    nodes, capacity, per_node = sizes
    offset = ids - node
    offset = jnp.where(offset < 0, offset + nodes, offset)
    place = jnp.where(placed >= 0, offset * per_node + micro_batch * capacity + placed, -1)
    return [slot == place[k : k + 1, :] for k in range(ids.shape[0])]


def slots_kernel(slot_ref):
    slot_ref[...] = lax.broadcasted_iota(jnp.int32, slot_ref.shape, 0)


def pass_kernel(in_ref, out_ref):
    out_ref[...] = in_ref[...]


def dispatch_kernel(
    sizes, node_size, slot_ref, hidden_ref, gain_ref, ids_ref, placed_ref, own_ref, rest_ref
):
    node = lax.axis_index("ep") // node_size
    gain = gain_ref[...].astype(F32).reshape(1, -1)
    slots = 0.0
    for m in range(hidden_ref.shape[0]):
        flags = hits(ids_ref[m], placed_ref[m], slot_ref[...], sizes, node, m)
        picks = jnp.where(functools.reduce(jnp.logical_or, flags), 1.0, 0.0).astype(BF16)
        values = hidden_ref[m].astype(F32)
        scale = lax.rsqrt(jnp.mean(values * values, axis=-1, keepdims=True) + 1e-06)
        normed = (values * scale * gain).astype(BF16)
        slots = slots + jnp.dot(picks, normed, preferred_element_type=F32)
    per_node = own_ref.shape[0]
    own_ref[...] = slots[:per_node].astype(BF16)
    rest_ref[...] = slots[per_node:].astype(BF16)


def table_kernel(sizes, node_size, slot_ref, ids_ref, placed_ref, shares_ref, table_ref):
    node = lax.axis_index("ep") // node_size
    for m in range(ids_ref.shape[0]):
        flags = hits(ids_ref[m], placed_ref[m], slot_ref[...], sizes, node, m)
        table = sum(
            jnp.where(flag, shares_ref[m][k : k + 1, :], 0.0) for k, flag in enumerate(flags)
        )
        table_ref[m] = table.T


def join_kernel(own_ref, rest_ref, out_ref):
    out_ref[...] = jnp.concatenate([own_ref[...].astype(F32), rest_ref[...].astype(F32)], 0).astype(
        BF16
    )


def hidden_units(pieces, gate_ref, up_ref):
    rows = jnp.concatenate([ref[...].astype(F32) for ref in pieces], 0).astype(BF16)
    gate_val = jnp.dot(rows, gate_ref[...], preferred_element_type=F32)
    up_val = jnp.dot(rows, up_ref[...], preferred_element_type=F32)
    return gate_val / (1.0 + jnp.exp(-gate_val)) * up_val


def early_kernel(*refs):
    refs[-1][...] = hidden_units(refs[:-3], *refs[-3:-1])


def down_halves(active, down_ref, keep_ref, send_ref):
    core = lax.axis_index("tp")
    half = keep_ref.shape[1]

    def down(which):
        columns = pl.ds(pl.multiple_of(which * half, 128), half)
        return jnp.dot(active, down_ref[:, columns], preferred_element_type=F32)

    send_ref[...] = down(1 - core).astype(BF16)
    keep_ref[...] = down(core)


def expert_kernel(*refs):
    pieces, (gate_ref, up_ref, early_ref, down_ref, keep_ref, send_ref) = refs[:-6], refs[-6:]
    late = hidden_units(pieces, gate_ref, up_ref)
    active = jnp.concatenate([early_ref[...], late], 0).astype(BF16)
    down_halves(active, down_ref, keep_ref, send_ref)


def own_or_rest(own, rest):
    return jnp.where(lax.axis_index("tp") == 0, own, rest)


def chip_product(rows, weight_refs):
    total = 0.0
    for gate_ref, up_ref, down_ref in (weight_refs[:3], weight_refs[3:]):
        gate_val = jnp.dot(rows, gate_ref[...], preferred_element_type=F32)
        up_val = jnp.dot(rows, up_ref[...], preferred_element_type=F32)
        active = (gate_val / (1.0 + jnp.exp(-gate_val)) * up_val).astype(BF16)
        total = total + jnp.dot(active, down_ref[...], preferred_element_type=F32)
    return total


def chip_kernel(hop_ref, passed_ref, side_ref, own_ref, two_ref, *refs):
    weight_refs, (hop_out, passed_out, side_out, own_out, two_out) = refs[:6], refs[6:]
    count = hop_ref.shape[0]
    hop, passed, side, own, two = (
        ref[...].astype(F32) for ref in (hop_ref, passed_ref, side_ref, own_ref, two_ref)
    )
    rows = jnp.concatenate([hop, passed, side, own_or_rest(own, two)], 0).astype(BF16)
    total = chip_product(rows, weight_refs)
    hop_out[...] = total[:count]
    passed_out[...] = total[count : 2 * count].astype(BF16)
    side_out[...] = total[2 * count : 3 * count].astype(BF16)
    own_out[...] = total[3 * count :]
    two_out[...] = total[3 * count :].astype(BF16)


def halves_kernel(own_ref, two_ref, side_ref, back_ref, own_out, back_out, send_ref):
    core = lax.axis_index("tp")
    half = back_out.shape[1]

    def columns(which):
        block = pl.ds(pl.multiple_of(which * half, 128), half)
        own = own_or_rest(own_ref[:, block], two_ref[:, block].astype(F32))
        return own + side_ref[:, block].astype(F32), back_ref[:, block].astype(F32)

    own_out[...], back_out[...] = columns(core)
    send_ref[...] = jnp.concatenate(columns(1 - core), 0).astype(BF16)


def base_kernel(sizes, hidden_ref, table_ref, own_ref, back_ref, out_ref):
    own, back = own_ref[...], back_ref[...]
    half = out_ref.shape[2]
    columns = pl.ds(pl.multiple_of(lax.axis_index("tp") * half, 128), half)
    for m in range(hidden_ref.shape[0]):
        base = hidden_ref[m, :, columns].astype(F32)
        base = weighted(base, table_ref[m], own, sizes, m, 0, 1)
        out_ref[m] = weighted(base, table_ref[m], back, sizes, m, 1, 1)


def last_kernel(sizes, base_ref, table_ref, got_ref, out_ref):
    got = got_ref[...].astype(F32)
    count = got.shape[0] // 2
    for m in range(base_ref.shape[0]):
        base = weighted(base_ref[m], table_ref[m], got[:count], sizes, m, 0, 1)
        out_ref[m] = weighted(base, table_ref[m], got[count:], sizes, m, 1, 1).astype(BF16)


def add_cores_kernel(keep_ref, got_ref, *out_refs):
    total = keep_ref[...] + got_ref[...].astype(F32)
    start = 0
    for ref in out_refs:
        ref[...] = total[start : start + ref.shape[0]].astype(ref.dtype)
        start += ref.shape[0]


def add_members_kernel(*refs):
    count = refs[-1].shape[0]
    total = refs[0][...]
    for ref in refs[1:-1]:
        block = ref[...].astype(F32)
        total = total + block[block.shape[0] - count :]
    refs[-1][...] = total.astype(BF16)


def weighted(base, weights, block, sizes, micro_batch, first, count):
    nodes, capacity, per_node = sizes
    for n in range(count):
        for c in range(capacity):
            slot = n * per_node + micro_batch * capacity + c
            column = first * per_node + slot
            base = base + weights[:, column : column + 1] * block[slot : slot + 1, :]
    return base


def own_kernel(sizes, hidden_ref, weights_ref, *refs):
    own_refs, out_ref = refs[:-1], refs[-1]
    own = own_refs[0][...]
    for ref in own_refs[1:]:
        own = own + ref[...].astype(F32)[: own.shape[0]]
    half = out_ref.shape[2]
    columns = pl.ds(pl.multiple_of(lax.axis_index("tp") * half, 128), half)
    for m in range(hidden_ref.shape[0]):
        base = hidden_ref[m, :, columns].astype(F32)
        out_ref[m] = weighted(base, weights_ref[m], own, sizes, m, 0, 1)


def rest_kernel(sizes, base_ref, weights_ref, rest_ref, out_ref):
    rest = rest_ref[...].astype(F32)
    for m in range(base_ref.shape[0]):
        out_ref[m] = weighted(base_ref[m], weights_ref[m], rest, sizes, m, 1, sizes[0] - 1).astype(
            BF16
        )


def per_device(hidden, norm_gain, expert_ids, shares, slot_index, w_gate, w_up, w_down):
    micro_count, row_count, model_width = hidden.shape
    top_count = expert_ids.shape[2]
    ep_count = lax.axis_size("ep")
    share_count = lax.axis_size("tp")
    node_size = FF // SLICE // share_count
    nodes = ep_count // node_size
    capacity = row_count * top_count // nodes
    half = model_width // share_count
    per_node = micro_count * capacity
    all_rows = nodes * per_node
    rest_rows = all_rows - per_node
    sizes = (nodes, capacity, per_node)
    ids, placed, weights = (jnp.swapaxes(a, 1, 2) for a in (expert_ids, slot_index, shares))
    small = all_rows <= 32
    params = pltpu.CompilerParams(vmem_limit_bytes=(16 if small else 56) * 1024 * 1024)

    def call(kernel, outs, *args, scratch=(), cost=0):
        return pl.pallas_call(
            kernel,
            out_shape=[jax.ShapeDtypeStruct(shape, kind) for shape, kind in outs],
            scratch_shapes=scratch,
            compiler_params=params,
            cost_estimate=pl.CostEstimate(flops=cost, bytes_accessed=cost // 500, transcendentals=0),
        )(*args)

    def to_member(array, k):
        pairs = [(j, j // node_size * node_size + (j % node_size ^ k)) for j in range(ep_count)]
        return lax.ppermute(array, "ep", pairs)

    def to_nodes(array, sign):
        blocks = []
        for n in range(1, nodes):
            block = array if nodes == 2 else array[(n - 1) * per_node : n * per_node]
            pairs = [(j, (j + sign * n * node_size) % ep_count) for j in range(ep_count)]
            blocks.append(lax.ppermute(block, "ep", pairs))
        return blocks[0] if nodes == 2 else jnp.concatenate(blocks, 0)

    (slot,) = call(slots_kernel, [((all_rows, row_count), jnp.int32)], cost=5 * 10**9)
    own, rest = call(
        functools.partial(dispatch_kernel, sizes, node_size),
        [((per_node, model_width), BF16), ((rest_rows, model_width), BF16)],
        slot,
        hidden,
        norm_gain,
        ids,
        placed,
        cost=20 * 10**9,
    )
    (table,) = call(
        functools.partial(table_kernel, sizes, node_size),
        [((micro_count, row_count, all_rows), F32)],
        slot,
        ids,
        placed,
        weights,
    )
    block = (node_size * all_rows, half)

    def early_rows(*pieces):
        shape = (sum(piece.shape[0] for piece in pieces), w_gate.shape[1])
        (early,) = call(early_kernel, [(shape, F32)], *pieces, w_gate, w_up, cost=4 * 10**9)
        return early

    if nodes == 2 and node_size == 4 and share_count == 2:

        def by_core(array, flip_zero, flip_one):
            pairs = []
            for j in range(ep_count):
                pairs += [(2 * j, 2 * (j ^ flip_zero)), (2 * j + 1, 2 * (j ^ flip_one) + 1)]
            return lax.ppermute(array, ("ep", "tp"), pairs)

        swap = [(0, 1), (1, 0)]
        full, narrow = (per_node, model_width), (per_node, half)
        weights = [w_gate, w_up, w_down]
        weights += [lax.ppermute(array, "tp", swap) for array in weights]
        hop = by_core(rest, node_size, node_size ^ 2)
        two, side = to_member(own, 2), by_core(own, 1, 3)
        (hop,) = call(pass_kernel, [(full, BF16)], hop, cost=20 * 10**9)
        passed = to_member(hop, 1)
        hop, passed, side, own, two = call(
            chip_kernel,
            [(full, F32), (full, BF16), (full, BF16), (full, F32), (full, BF16)],
            hop,
            passed,
            side,
            own,
            two,
            *weights,
            cost=10**6,
        )
        passed = to_member(passed, 1)
        side, two = by_core(side, 1, 3), to_member(two, 2)
        (outbox,) = call(add_members_kernel, [(full, BF16)], hop, passed)
        back = by_core(outbox, node_size, node_size ^ 2)
        own, back, send = call(
            halves_kernel,
            [(narrow, F32), (narrow, F32), ((2 * per_node, half), BF16)],
            own,
            two,
            side,
            back,
        )
        got = lax.ppermute(send, "tp", swap)
        rows = (micro_count, row_count, half)
        (base,) = call(
            functools.partial(base_kernel, sizes),
            [(rows, F32)],
            hidden,
            table,
            own,
            back,
        )
        (mixed,) = call(functools.partial(last_kernel, sizes), [(rows, BF16)], base, table, got)
        return mixed

    names = ("own", "own_one", "own_two", "rest", "rest_one", "rest_two", "own_far", "rest_far")
    inbox = to_nodes(rest, 1)
    own_one, own_two = to_member(own, 1), to_member(own, 2)
    (joined,) = call(join_kernel, [((all_rows, model_width), BF16)], own, inbox)
    far = to_member(joined, 3)
    rest_two, rest_one = to_member(inbox, 2), to_member(inbox, 1)
    early = early_rows(own, own_one, own_two)
    keep, send = call(
        expert_kernel,
        [(block, F32), (block, BF16)],
        inbox,
        rest_one,
        rest_two,
        far,
        w_gate,
        w_up,
        early,
        w_down,
        cost=10**6,
    )
    got = lax.ppermute(send, "tp", [(i, (i + 1) % share_count) for i in range(share_count)])
    narrow, wide = (per_node, half), (rest_rows, half)
    shapes = [
        (narrow if name.startswith("own") else wide, F32 if name in ("own", "rest") else BF16)
        for name in names
    ]
    sums = dict(zip(names, call(add_cores_kernel, shapes, keep, got)))
    own, own_one, own_two, own_far = (sums[n] for n in ("own", "own_one", "own_two", "own_far"))
    rest, rest_one, rest_two, rest_far = (
        sums[n] for n in ("rest", "rest_one", "rest_two", "rest_far")
    )
    rest_far, rest_two = to_member(rest_far, 3), to_member(rest_two, 2)
    (near,) = call(join_kernel, [((all_rows, half), BF16)], own_one, rest_one)
    near = to_member(near, 1)
    own_far, own_two = to_member(own_far, 3), to_member(own_two, 2)
    home = [own, near, own_far, own_two]
    (outbox,) = call(add_members_kernel, [(wide, BF16)], rest, rest_far, rest_two, near)
    returned = to_nodes(outbox, -1)
    rows = (micro_count, row_count, half)
    (base,) = call(functools.partial(own_kernel, sizes), [(rows, F32)], hidden, table, *home)
    (mixed,) = call(functools.partial(rest_kernel, sizes), [(rows, BF16)], base, table, returned)
    return mixed


def solution(mesh):
    in_specs = (
        P(None, ("groups", "ep"), None),
        P(),
        P(None, ("groups", "ep"), None),
        P(None, ("groups", "ep"), None),
        P(None, ("groups", "ep"), None),
        P(None, ("ep", "tp")),
        P(None, ("ep", "tp")),
        P(("ep", "tp"), None),
    )
    out_specs = P(None, ("groups", "ep"), "tp")
    return jax.shard_map(
        per_device, mesh=mesh, in_specs=in_specs, out_specs=out_specs, check_vma=False
    )
```
